32 devices in a mesh: gx: 8 (over z, y), gy: 2 (over x), gz: 2 (over core).
Axes of the slice: x: 2, y: 2, z: 4, core: 2. Of those that a mesh axis runs over, the one named last changes fastest.
Arguments:
- pops: float32 [19, 32, 64, 256], P(None, 'gz', 'gx', 'gy'), as said below
- solid: int32 [32, 64, 256], P('gz', 'gx', 'gy'), may hold values 0 or 1
- surf_cell: int32 [2, 8, 2, 512], P('gz', 'gx', 'gy'), may hold values from 0 to 16383
- surf_panel: int32 [2, 8, 2, 512], P('gz', 'gx', 'gy'), may hold values from -1 to 39, as said below
- surf_area: float32 [2, 8, 2, 512], P('gz', 'gx', 'gy'), may hold values from 0.1 to 1
- mode_shape: float32 [2, 8, 2, 12, 512], P('gz', 'gx', 'gy'), may hold values from -5 to 5
- mode_of_panel: int32 [40], replicated, may hold values from 0 to 11
- compliance: float32 [12], replicated, may hold values from 0.3 to 3
Outputs:
- read: float32 [19, 32, 64, 256], P(None, 'gz', 'gx', 'gy')
- panel_force: float32 [40], replicated
- mode_amplitude: float32 [12], replicated
The draws below stay inside these ranges and needn't reach their ends.
Inputs may be any that keep to these rules, and one draw needn't show every extreme that they name: pops is positive, with densities near 1 and flow speeds below 0.25. `surf_panel`: -1 marks an empty slot; on each device the live slots come first, at least 64 of them; some device has all 512 slots live; one panel's surfels lie on at most about 40 consecutive bricks in the linear order (vertical, streamwise, crosswise) of the devices, counted periodically so that the last brick is followed by the first.
All inputs are finite; a program needn't handle non-finite values. No bound on the sum of `solid` on one device may be relied on, other than what follows from the above.
Results may differ from the reference program's by a relative error of at most 0.00011.
Values sent between devices are 32-bit elements; how exact they have to be, the bound alone decides.
A program may use at most 64 MiB of HBM per device.

```python
import math
import jax
import jax.numpy as jnp

PANELS = 40
MODES = 12
CZ = 16
CX = 8
CY = 128
S_DEV = 512
NZ = 32
NX = 64
NY = 256
N_GX = 8
N_GY = 2
N_GZ = 2


VELOCITY = ((0, 0, 0), (1, 0, 0), (-1, 0, 0), (0, 1, 0), (0, -1, 0), (0, 0, 1), (0, 0, -1), (1, 1, 0), (-1, -1, 0), (1, -1, 0), (-1, 1, 0), (1, 0, 1), (-1, 0, -1), (1, 0, -1), (-1, 0, 1), (0, 1, 1), (0, -1, -1), (0, 1, -1), (0, -1, 1))


WEIGHTS = (1.0 / 3.0,) + (1.0 / 18.0,) * 6 + (1.0 / 36.0,) * 12


def draw_pops(key, part):
    shape3 = (NZ, NX, NY)
    keys = jax.random.split(key, 5)
    density = 1.0 + 0.05 * jax.random.truncated_normal(keys[0], -4.0, 4.0, shape3, jnp.float32)
    flows = [0.04 * jax.random.truncated_normal(keys[1 + axis], -4.0, 4.0, shape3, jnp.float32) for axis in range(3)]
    squared = flows[0] * flows[0] + flows[1] * flows[1] + flows[2] * flows[2]
    noise = jax.random.truncated_normal(keys[4], -4.0, 4.0, (19,) + shape3, jnp.float32)
    result = []
    for index in range(19):
        vel = VELOCITY[index]
        projected = vel[0] * flows[0] + vel[1] * flows[1] + vel[2] * flows[2]
        equilib = WEIGHTS[index] * density * (1.0 + 3.0 * projected + 4.5 * projected * projected - 1.5 * squared)
        result.append(equilib + 0.005 * WEIGHTS[index] * noise[index])
    return jnp.stack(result).astype(jnp.float32)


def draw_surf_panel(key, part):
    ndev = N_GZ * N_GX * N_GY
    linear = jnp.arange(ndev, dtype=jnp.int32).reshape(N_GZ, N_GX, N_GY, 1)
    first, second = jax.random.split(key, 2)
    base = linear * PANELS // ndev
    offset = jax.random.randint(first, (N_GZ, N_GX, N_GY, S_DEV), 0, 3, jnp.int32)
    slot = jnp.arange(S_DEV, dtype=jnp.int32)
    offset = jnp.where(slot == 0, 0, offset)
    panel = (base + offset) % PANELS
    live_count = jax.random.randint(second, (N_GZ, N_GX, N_GY, 1), S_DEV // 8, S_DEV + 1, jnp.int32)
    live_count = jnp.where(linear == 0, S_DEV, live_count)
    live_count = jnp.where(linear == ndev - 1, S_DEV // 8, live_count)
    return jnp.where(slot < live_count, panel, -1).astype(jnp.int32)


def plant(entries, rng, smallest, largest):
    extent = entries.shape
    place = [jax.random.randint(jax.random.fold_in(rng, axis), (), 0, extent[axis]) for axis in range(len(extent))]
    entries = entries.at[tuple(place)].set(smallest)
    longest = extent.index(max(extent))
    place[longest] = (place[longest] + 1) % extent[longest]
    return entries.at[tuple(place)].set(largest)


def level_of(stream_key, shape, pieces, least, high):
    factor_of, own = 1.0, jax.random.fold_in(stream_key, 6)
    for dim, parts in pieces:
        heights = jnp.exp(jax.random.uniform(jax.random.fold_in(own, dim), (parts,), jnp.float32, least / len(pieces), high / len(pieces)))
        factor_of = factor_of * jnp.repeat(heights, shape[dim] // parts).reshape([-1 if axis == dim else 1 for axis in range(len(shape))])
    return factor_of


def bell_draw(stream_key, dims, width, limit, cuts=(), kind=jnp.bfloat16):
    values = jax.random.normal(stream_key, dims, jnp.float32) * width
    if len(cuts) > 0:
        values = level_of(stream_key, dims, cuts, -0.22, 0.18) * values
    return jnp.clip(values, min=-limit, max=limit).astype(kind)


def setup_inputs(seed: int = 0) -> dict:
    seeds = jax.random.split(jax.random.key(seed), 9)
    pops = draw_pops(jax.random.fold_in(seeds[8], 71), 0)
    solid = plant((jax.random.randint(seeds[1], (NZ, NX, NY), 0, 8) < 1).astype(jnp.int32), jax.random.fold_in(seeds[1], 1), 0, 1)
    surf_cell = plant(jax.random.randint(seeds[2], (N_GZ, N_GX, N_GY, S_DEV), 0, CZ * CX * CY), jax.random.fold_in(seeds[2], 1), 0, (CZ * CX * CY) - 1).astype(jnp.int32)
    surf_panel = draw_surf_panel(jax.random.fold_in(seeds[8], 71), 0)
    surf_area = jnp.clip(jnp.exp(math.log(1.0) - 2.3025851 * jax.random.uniform(seeds[4], (N_GZ, N_GX, N_GY, S_DEV), jnp.float32) ** level_of(seeds[4], (N_GZ, N_GX, N_GY, S_DEV), ((0, 2), (1, 8), (2, 2)), -0.2, 0.2)), 0.1, 1.0)
    mode_shape = bell_draw(seeds[5], (N_GZ, N_GX, N_GY, MODES, S_DEV), 1.0, 5.0, ((0, 2), (1, 8), (2, 2)), jnp.float32)
    mode_of_panel = plant(jax.random.randint(seeds[6], (PANELS,), 0, MODES), jax.random.fold_in(seeds[6], 1), 0, MODES - 1).astype(jnp.int32)
    compliance = jnp.clip(jnp.exp(jax.random.uniform(seeds[7], (MODES,), jnp.float32, math.log(0.3), math.log(3.0))), 0.3, 3.0)
    return {"pops": pops, "solid": solid, "surf_cell": surf_cell, "surf_panel": surf_panel, "surf_area": surf_area, "mode_shape": mode_shape, "mode_of_panel": mode_of_panel, "compliance": compliance}


VELOCITY = ((0, 0, 0), (1, 0, 0), (-1, 0, 0), (0, 1, 0), (0, -1, 0), (0, 0, 1), (0, 0, -1),
            (1, 1, 0), (-1, -1, 0), (1, -1, 0), (-1, 1, 0), (1, 0, 1), (-1, 0, -1),
            (1, 0, -1), (-1, 0, 1), (0, 1, 1), (0, -1, -1), (0, 1, -1), (0, -1, 1))
WEIGHTS = (1.0 / 3.0,) + (1.0 / 18.0,) * 6 + (1.0 / 36.0,) * 12
OPPOSITE = (0, 2, 1, 4, 3, 6, 5, 8, 7, 10, 9, 12, 11, 14, 13, 16, 15, 18, 17)
OMEGA = 1.0 / 0.6
WALL_SCALE = 0.02


def collide(pops, solid):
    density = pops[0]
    for index in range(1, 19):
        density = density + pops[index]
    moments = []
    for axis in range(3):
        total = jnp.zeros_like(density)
        for index in range(19):
            comp = VELOCITY[index][axis]
            if comp == 1:
                total = total + pops[index]
            elif comp == -1:
                total = total - pops[index]
        moments.append(total / density)
    squared = moments[0] * moments[0] + moments[1] * moments[1] + moments[2] * moments[2]
    result = []
    for index in range(19):
        projected = jnp.zeros_like(density)
        for axis in range(3):
            comp = VELOCITY[index][axis]
            if comp == 1:
                projected = projected + moments[axis]
            elif comp == -1:
                projected = projected - moments[axis]
        equilib = WEIGHTS[index] * density * (1.0 + 3.0 * projected + 4.5 * projected * projected - 1.5 * squared)
        relaxed = pops[index] + OMEGA * (equilib - pops[index])
        result.append(jnp.where(solid == 1, pops[OPPOSITE[index]], relaxed))
    return density, result


def reference(pops, solid, surf_cell, surf_panel, surf_area, mode_shape, mode_of_panel, compliance):
    density, post = collide(pops, solid)
    ndev = N_GZ * N_GX * N_GY
    cells = CZ * CX * CY
    bricks = density.reshape(N_GZ, CZ, N_GX, CX, N_GY, CY).transpose(0, 2, 4, 1, 3, 5).reshape(ndev, cells)
    cell_rows = surf_cell.reshape(ndev, S_DEV)
    panel_rows = surf_panel.reshape(ndev, S_DEV)
    gathered = jnp.take_along_axis(bricks, cell_rows, axis=1)
    live = panel_rows >= 0
    contrib = jnp.where(live, surf_area.reshape(ndev, S_DEV) * ((gathered - 1.0) / 3.0), 0.0)
    panel_ids = jnp.arange(PANELS, dtype=jnp.int32)
    panel_force = jnp.sum(jnp.where(panel_rows[:, :, None] == panel_ids, contrib[:, :, None], 0.0), axis=(0, 1))
    mode_ids = jnp.arange(MODES, dtype=jnp.int32)
    mode_load = jnp.sum(jnp.where(mode_of_panel[:, None] == mode_ids[None, :], panel_force[:, None], 0.0), axis=0)
    mode_amplitude = compliance * mode_load
    shapes = mode_shape.reshape(ndev, MODES, S_DEV)
    wall = WALL_SCALE * jnp.sum(mode_amplitude[None, :, None] * shapes, axis=1)
    values = jnp.where(live, gathered * wall, 0.0)
    rows = jnp.arange(ndev, dtype=jnp.int32)[:, None]
    flux_bricks = jnp.zeros((ndev, cells), jnp.float32).at[rows, cell_rows].add(values)
    wall_flux = flux_bricks.reshape(N_GZ, N_GX, N_GY, CZ, CX, CY).transpose(0, 3, 1, 4, 2, 5).reshape(NZ, NX, NY)
    read = []
    for index in range(19):
        coef = 6.0 * WEIGHTS[index] * VELOCITY[index][0]
        corrected = post[index] + coef * wall_flux
        vel = VELOCITY[index]
        read.append(jnp.roll(corrected, (vel[2], vel[0], vel[1]), axis=(0, 1, 2)))
    return jnp.stack(read), panel_force, mode_amplitude
```

```python
import functools

import jax
import jax.numpy as jnp
from jax import lax
from jax.experimental import pallas as pl
from jax.experimental.pallas import tpu as pltpu
from jax.sharding import PartitionSpec as P

PANELS = 40
MODES = 12
VELOCITY = (
    (0, 0, 0),
    (1, 0, 0),
    (-1, 0, 0),
    (0, 1, 0),
    (0, -1, 0),
    (0, 0, 1),
    (0, 0, -1),
    (1, 1, 0),
    (-1, -1, 0),
    (1, -1, 0),
    (-1, 1, 0),
    (1, 0, 1),
    (-1, 0, -1),
    (1, 0, -1),
    (-1, 0, 1),
    (0, 1, 1),
    (0, -1, -1),
    (0, 1, -1),
    (0, -1, 1),
)
WEIGHTS = (1.0 / 3.0,) + (1.0 / 18.0,) * 6 + (1.0 / 36.0,) * 12
OMEGA = 1.0 / 0.6
WALL_SCALE = 0.02
COEF = tuple(6.0 * w * v[0] for w, v in zip(WEIGHTS, VELOCITY))
SIGNS = (1, -1)


def moving(axis, sign):
    return tuple(i for i in range(19) if VELOCITY[i][axis] == sign)


X_GROUP = tuple(moving(0, s) for s in SIGNS)
Y_GROUP = tuple(moving(1, s) for s in SIGNS)
Z_GROUP = tuple(moving(2, s) for s in SIGNS)
ORDER = Z_GROUP[0] + Z_GROUP[1] + tuple(i for i in range(19) if VELOCITY[i][2] == 0)
PLACE = tuple(ORDER.index(i) for i in range(19))
AXES = ("gx", "gy", "gz")
MESH = pl.DeviceIdType.MESH
N_LOADS = 4
MODE_ROWS = 16
CELL_ROW = MODES
LOW, HIGH = 16, 17
F32 = jnp.float32
BF16 = jnp.bfloat16


def stages_of(sizes):
    if sizes[0] * sizes[1] * sizes[2] <= 64:
        return (AXES,)
    return (("gx",), ("gy", "gz"))


def halves(x):
    high = x.astype(BF16)
    return high, (x - high.astype(F32)).astype(BF16)


def dot(a, b):
    return jnp.dot(a, b, preferred_element_type=F32)


def dot_nt(a, b):
    return lax.dot_general(a, b, (((1,), (1,)), ((), ())), preferred_element_type=F32)


def stage_offsets(stage, sizes):
    result = [(0, 0, 0)]
    for dim, axis in enumerate(AXES):
        if axis in stage:
            result = [
                tuple(k if d == dim else o[d] for d in range(3))
                for o in result
                for k in range(sizes[dim])
            ]
    return [o for o in result if o != (0, 0, 0)]


def offsets_of(sizes):
    found = []
    for i in range(1, 19):
        found.append(tuple(c % n for c, n in zip(VELOCITY[i], sizes)))
    for stage in stages_of(sizes):
        found += stage_offsets(stage, sizes)
    return sorted(set(found))


def tree_sum(terms):
    while len(terms) > 1:
        terms = [sum(terms[k + 1 : k + 2], terms[k]) for k in range(0, len(terms), 2)]
    return terms[0]


N_HALO = 18 + 4
N_SURF = 2 + 4 + 2 + 4 + 2


def exchange(
    sizes,
    pops_in,
    solid_in,
    cell_in,
    panel_in,
    area_in,
    shapes_in,
    panel_mode_in,
    compliance_in,
    pre,
    flux_m,
    flux_x,
    flux_y,
    flux_c,
    total_out,
    drive_out,
    pops,
    solid,
    cell,
    panel,
    area,
    shape_rows,
    panel_mode,
    compliance,
    mine,
    load_sem,
    post,
    dens,
    xs,
    xh,
    ys,
    yh,
    yxh,
    yzh,
    theirs,
    edges,
    edges_in,
    faces,
    faces_in,
    corners,
    corners_in,
    surf_send,
    surf_recv,
    slots,
    send_sem,
    recv_sem,
    stage_send,
    stage_recv,
):
    depth, rows, width = pops.shape[1:]
    cells = depth * rows
    groups = width // depth
    here = tuple(lax.axis_index(a) for a in AXES)
    stages = stages_of(sizes)
    targets = {}

    def at(offset):
        key = tuple(o % n for o, n in zip(offset, sizes))
        if key not in targets:
            targets[key] = tuple(
                lax.rem(h + o, n) if o else h for h, o, n in zip(here, key, sizes)
            )
        return targets[key]

    partners = offsets_of(sizes)
    barrier = pltpu.get_barrier_semaphore()
    for offset in partners:
        pl.semaphore_signal(barrier, inc=1, device_id=at(offset), device_id_type=MESH)

    small = [(cell_in, cell), (panel_in, panel), (area_in, area), (shapes_in, shape_rows)]
    part = depth // N_LOADS
    cuts = [pl.ds(n * part, part) for n in range(N_LOADS)]
    big = [(pops_in.at[:, c], pops.at[:, c]) for c in cuts]
    late = [(solid_in, solid), (panel_mode_in, panel_mode), (compliance_in, compliance)]
    loads = []
    for n, (src, dst) in enumerate(small + big + late):
        loads.append(pltpu.make_async_copy(src, dst, load_sem.at[n]))
        loads[n].start()

    lane = lax.broadcasted_iota(jnp.int32, (rows, width), 1)
    sub = lax.broadcasted_iota(jnp.int32, (rows, width), 0)

    for copy in loads[: len(small)]:
        copy.wait()
    n_surf = cell.shape[1]
    live = panel[...] >= 0
    col = lax.rem(cell[...], width)
    row = lax.div(cell[...], width)
    cell_x = lax.rem(row, rows)
    cell_z = lax.div(row, rows)
    spot = lax.broadcasted_iota(jnp.int32, (width, n_surf), 0)
    pick_col = jnp.where(spot == col, 1.0, 0.0).astype(BF16)
    on_row = lax.broadcasted_iota(jnp.int32, (cells, n_surf), 0) == row

    for m in range(MODES):
        mine[m : m + 1, :] = jnp.where(live, shape_rows[m] * WALL_SCALE, 0.0)
    mine[CELL_ROW : CELL_ROW + 1, :] = cell[...].astype(F32)
    mine[CELL_ROW + 1 :, :] = jnp.zeros((MODE_ROWS - CELL_ROW - 1, n_surf), F32)

    table = mine[...]
    masked = []
    for a in range(2):
        on_x = cell_x == (rows - 1 if a == 0 else 0)
        for b in range(2):
            on_z = cell_z == (depth - 1 if b == 0 else 0)
            masked.append(jnp.where(on_x & on_z, table, 0.0))
    high, low = halves(jnp.concatenate(masked, axis=0))
    edge_rows = dot_nt(high, pick_col) + dot_nt(low, pick_col)
    for k in range(4):
        edges[k // 2, k % 2] = edge_rows[k * MODE_ROWS : (k + 1) * MODE_ROWS]
    row_id = lax.broadcasted_iota(jnp.int32, (rows, n_surf), 0)
    sides = jnp.concatenate(
        [
            jnp.where((row_id == cell_x) & (col == (width - 1 if a == 0 else 0)), 1.0, 0.0)
            for a in range(2)
        ],
        axis=0,
    ).astype(BF16)
    on_z = lax.rem(spot, depth) == cell_z
    for t in range(2):
        spread_rows = jnp.concatenate(
            [
                jnp.broadcast_to(
                    table[t * groups + g : t * groups + g + 1, :]
                    if t * groups + g < MODES
                    else jnp.zeros((1, n_surf), F32),
                    (depth, n_surf),
                )
                for g in range(groups)
            ],
            axis=0,
        )
        high, low = halves(jnp.where(on_z, spread_rows, 0.0))
        packed = dot_nt(sides, high) + dot_nt(sides, low)
        for a in range(2):
            faces[a, t] = packed[a * rows : (a + 1) * rows]
            for b in range(2):
                edge = a * rows + (rows - 1 if b == 0 else 0)
                corners[a, b, t] = packed[edge : edge + 1]

    def add_up(z, carry):
        density = pops[0, z]
        for i in range(1, 19):
            density = density + pops[i, z]
        dens[z] = density
        return carry

    for n in range(N_LOADS):
        loads[len(small) + n].wait()
        lax.fori_loop(n * part, (n + 1) * part, add_up, 0, unroll=True)
    gauge_high, gauge_low = halves(dens[...].reshape(cells, width) - 1.0)
    by_row = dot(gauge_high, pick_col) + dot(gauge_low, pick_col)
    excess = jnp.sum(jnp.where(on_row, by_row, 0.0), axis=0, keepdims=True)
    contrib = jnp.where(live, area[...] * (excess / 3.0), 0.0)
    pick_panel = jnp.where(spot == panel[...], 1.0, 0.0).astype(BF16)
    contrib_high, contrib_low = halves(jnp.broadcast_to(contrib, (8, n_surf)))
    partial = dot_nt(contrib_high, pick_panel) + dot_nt(contrib_low, pick_panel)
    partial = partial[0:1]

    pl.semaphore_wait(barrier, len(partners))

    def stage_start(n, value):
        stage = stages[n]
        index = 0
        for dim, axis in enumerate(AXES):
            if axis in stage:
                index = index * sizes[dim] + here[dim]
        slots[n, index] = value
        for offset in stage_offsets(stage, sizes):
            pltpu.make_async_remote_copy(
                src_ref=slots.at[n, index],
                dst_ref=slots.at[n, index],
                send_sem=stage_send.at[n],
                recv_sem=stage_recv.at[n],
                device_id=at(offset),
                device_id_type=MESH,
            ).start()

    def stage_sum(n):
        count = len(stage_offsets(stages[n], sizes))
        whole = pltpu.make_async_remote_copy(
            src_ref=slots.at[n, pl.ds(0, count)],
            dst_ref=slots.at[n, pl.ds(0, count)],
            send_sem=stage_send.at[n],
            recv_sem=stage_recv.at[n],
            device_id=at(stage_offsets(stages[n], sizes)[0]),
            device_id_type=MESH,
        )
        whole.wait_recv()
        whole.wait_send()
        return tree_sum([slots[n, k] for k in range(count + 1)])

    stage_start(0, partial)

    surfels = []

    def pass_on(src, dst, offset):
        copy = pltpu.make_async_remote_copy(
            src_ref=src,
            dst_ref=dst,
            send_sem=surf_send.at[len(surfels)],
            recv_sem=surf_recv.at[len(surfels)],
            device_id=at(offset),
            device_id_type=MESH,
        )
        copy.start()
        surfels.append(copy)

    for a, s in enumerate(SIGNS):
        pass_on(mine, theirs.at[a], (s, 0, 0))
        pass_on(faces.at[a], faces_in.at[a], (0, s, 0))
        for b, t in enumerate(SIGNS):
            pass_on(edges.at[a, b], edges_in.at[a, b], (s, 0, t))
            pass_on(corners.at[a, b], corners_in.at[a, b], (t, s, 0))

    loads[len(small) + N_LOADS].wait()

    def collide(z, packed):
        f = [pops[i, z] for i in range(19)]
        density = dens[z]
        inverse = 1.0 / density
        u = []
        for axis in range(3):
            plus, minus = moving(axis, 1), moving(axis, -1)
            total = f[plus[0]] - f[minus[0]]
            for i, j in zip(plus[1:], minus[1:]):
                total = total + (f[i] - f[j])
            u.append(total * inverse)
        base = 1.0 - 1.5 * (u[0] * u[0] + u[1] * u[1] + u[2] * u[2])
        fixed = solid[z] == 1
        scaled = [OMEGA * w * density for w in WEIGHTS]
        new = [None] * 19
        new[0] = jnp.where(fixed, f[0], (1.0 - OMEGA) * f[0] + scaled[0] * base)
        for i in range(1, 19, 2):
            proj = None
            for axis in range(3):
                comp = VELOCITY[i][axis]
                if comp:
                    term = u[axis] if comp == 1 else -u[axis]
                    proj = term if proj is None else proj + term
            even = scaled[i] * (base + 4.5 * (proj * proj))
            odd = scaled[i] * (3.0 * proj)
            new[i] = jnp.where(fixed, f[i + 1], (1.0 - OMEGA) * f[i] + (even + odd))
            new[i + 1] = jnp.where(fixed, f[i], (1.0 - OMEGA) * f[i + 1] + (even - odd))
        for i in range(19):
            post[PLACE[i], z + 1] = new[i]
        packed = list(packed)
        for a in range(2):
            edge = rows - 1 if a == 0 else 0
            for k, i in enumerate(X_GROUP[a]):
                xs[a, k, z] = new[i][edge : edge + 1]
            xs[a, 5, z] = density[edge : edge + 1]
            edge = width - 1 if a == 0 else 0
            for j, value in enumerate([new[i] for i in Y_GROUP[a]] + [density]):
                column = jnp.broadcast_to(value[:, edge : edge + 1], (rows, width))
                packed[a] = jnp.where(lane == j * depth + z, column, packed[a])
        return tuple(packed)

    zero = jnp.zeros((rows, width), F32)
    packed = lax.fori_loop(0, depth, collide, (zero, zero))
    for a in range(2):
        ys[a] = packed[a]

    halo = []

    def send(src, dst, offset):
        copy = pltpu.make_async_remote_copy(
            src_ref=src,
            dst_ref=dst,
            send_sem=send_sem.at[len(halo)],
            recv_sem=recv_sem.at[len(halo)],
            device_id=at(offset),
            device_id_type=MESH,
        )
        copy.start()
        halo.append(copy)

    for a, s in enumerate(SIGNS):
        group = Z_GROUP[a]
        first = a * len(group)
        source, target = (depth, 0) if a == 0 else (1, depth + 1)
        send(xs.at[a], xh.at[a, :, pl.ds(1, depth)], (s, 0, 0))
        send(ys.at[a], yh.at[a], (0, s, 0))
        for b, t in enumerate(SIGNS):
            send(ys.at[a], yxh.at[a, b], (t, s, 0))
            send(ys.at[a], yzh.at[a, b], (0, s, t))
            k = [i for i in range(5) if VELOCITY[X_GROUP[a][i]][2] == t][0]
            edge, beyond = (depth - 1, 0) if b == 0 else (0, depth + 1)
            send(xs.at[a, k, edge], xh.at[a, k, beyond], (s, 0, t))
            send(xs.at[a, 5, edge], xh.at[a, 5, beyond], (s, 0, t))
        send(
            post.at[pl.ds(first, len(group)), source],
            post.at[pl.ds(first, len(group)), target],
            (0, 0, s),
        )

    in_row = jnp.where(on_row, 1.0, 0.0).astype(BF16).reshape(cells // 16, 16, n_surf)

    def scatter(m, carry):
        high, low = halves(jnp.broadcast_to(mine[pl.ds(m, 1), :], (16, n_surf)))
        flux = dot_nt((in_row * high[None]).reshape(cells, n_surf), pick_col)
        flux = flux + dot_nt((in_row * low[None]).reshape(cells, n_surf), pick_col)
        flux_m[m, pl.ds(1, depth)] = flux.reshape(depth, rows, width) * dens[...]
        return carry

    lax.fori_loop(0, MODES, scatter, 0)
    for a, s in enumerate(SIGNS):
        source, target = (depth, 0) if a == 0 else (1, depth + 1)
        pass_on(flux_m.at[:, source], flux_m.at[:, target], (0, 0, s))

    for copy in loads[len(small) + N_LOADS + 1 :]:
        copy.wait()
    mode_id = lax.broadcasted_iota(jnp.int32, (MODE_ROWS, PANELS), 0)
    diagonal = lax.broadcasted_iota(jnp.int32, (MODE_ROWS, MODES), 0) == lax.broadcasted_iota(
        jnp.int32, (MODE_ROWS, MODES), 1
    )
    factor = jnp.sum(jnp.where(diagonal, compliance[...], 0.0), axis=1, keepdims=True)
    drive_out[...] = jnp.where(panel_mode[...] == mode_id, factor, 0.0)

    for n in range(1, len(stages)):
        stage_start(n, stage_sum(n - 1))

    for copy in halo:
        copy.wait()

    columns = []
    for a in range(2):
        result = yh[a]
        for j, i in enumerate(Y_GROUP[a]):
            cx, _, cz = VELOCITY[i]
            own = (lane >= j * depth) & (lane < (j + 1) * depth)
            if cx:
                b = SIGNS.index(cx)
                edge = pltpu.roll(yxh[a, b], cx % rows, 0)
                whole = pltpu.roll(yh[a], cx % rows, 0)
                whole = jnp.where(sub == (0 if cx == 1 else rows - 1), edge, whole)
                result = jnp.where(own, whole, result)
            if cz:
                b = SIGNS.index(cz)
                whole = pltpu.roll(yh[a], cz % width, 1)
                wrapped = pltpu.roll(yzh[a, b], (-cz * (depth - 1)) % width, 1)
                place = j * depth if cz == 1 else (j + 1) * depth - 1
                whole = jnp.where(lane == place, wrapped, whole)
                result = jnp.where(own, whole, result)
        columns.append(result)

    def stream(z, columns):
        for i in range(19):
            cx, cy, cz = VELOCITY[i]
            source = z + 1 - cz
            value = post[PLACE[i], source]
            if cx:
                a = SIGNS.index(cx)
                line = xh[a, X_GROUP[a].index(i), source]
                value = pltpu.roll(value, cx % rows, 0)
                value = jnp.where(sub == (0 if cx == 1 else rows - 1), line, value)
            if cy:
                a = SIGNS.index(cy)
                j = Y_GROUP[a].index(i)
                value = pltpu.roll(value, cy % width, 1)
                column = jnp.broadcast_to(
                    columns[a][:, j * depth : j * depth + 1], (rows, width)
                )
                value = jnp.where(lane == (0 if cy == 1 else width - 1), column, value)
            pre[i, z] = value
        return tuple(pltpu.roll(c, width - 1, 1) for c in columns)

    lax.fori_loop(0, depth, stream, tuple(columns), unroll=2)

    for copy in surfels:
        copy.wait()

    def everywhere(tile, group):
        tile = jnp.where(lane // depth == group, tile, 0.0)
        step = depth
        while step < width:
            tile = tile + pltpu.roll(tile, step, 1)
            step *= 2
        return tile

    level_id = lax.broadcasted_iota(jnp.int32, (depth, n_surf), 0)
    for a in range(2):
        other = theirs[a, CELL_ROW : CELL_ROW + 1, :].astype(jnp.int32)
        pick = jnp.where(spot == lax.rem(other, width), 1.0, 0.0).astype(BF16)
        on_x = lax.rem(lax.div(other, width), rows) == (rows - 1 if a == 0 else 0)
        on_face = (level_id == lax.div(other, width * rows)) & on_x
        lines = jnp.concatenate(
            [jnp.where(on_face, theirs[a, m : m + 1, :], 0.0) for m in range(MODES)], axis=0
        )
        high, low = halves(lines)
        lines = dot_nt(high, pick) + dot_nt(low, pick)
        density = xh[a, 5, pl.ds(1, depth)].reshape(depth, width)
        for m in range(MODES):
            flux_x[a, m, 0:depth, :] = lines[m * depth : (m + 1) * depth] * density
        for b in range(2):
            place, slot = (LOW, 0) if b == 0 else (HIGH, depth + 1)
            line = xh[a, 5, slot]
            for m in range(MODES):
                flux_x[a, m, place : place + 1, :] = edges_in[a, b, m : m + 1, :] * line
        density = everywhere(yh[a], 5)
        for t in range(2):
            flux_y[a, t] = faces_in[a, t] * density
        for b in range(2):
            density = everywhere(yxh[a, b], 5)
            edge = rows - 1 if b == 0 else 0
            for t in range(2):
                k = 2 * a + b
                flux_c[t, k : k + 1, :] = corners_in[a, b, t] * density[edge : edge + 1]
    flux_c[:, 4:, :] = jnp.zeros((2, rows - 4, width), F32)
    for a in range(2):
        for m in range(MODES):
            flux_x[a, m, HIGH + 1 :, :] = jnp.zeros((rows - 2, width), F32)

    total_out[...] = stage_sum(len(stages) - 1)


MOVED = X_GROUP[0] + X_GROUP[1]
FIXED_RUNS = ((0, 1), (3, 4), (15, 4))
MOVED_RUNS = ((1, 2), (7, 8))
N_CUTS = 4


def apply(pre, flux_m, flux_x, flux_y, flux_c, total, drive, out, force_out, amp_out, stage, force, amplitude, sem):
    depth, rows, width = pre.shape[1:]
    copies = []

    def write(src, dst):
        copy = pltpu.make_async_copy(src, dst, sem.at[len(copies)])
        copy.start()
        copies.append(copy)

    for first, count in FIXED_RUNS:
        run = pl.ds(first, count)
        write(pre.at[run], out.at[run])

    lane = lax.broadcasted_iota(jnp.int32, (rows, width), 1)
    sub = lax.broadcasted_iota(jnp.int32, (rows, width), 0)
    load = total[:, :PANELS]
    force[...] = load
    write(force, force_out)
    amp = jnp.sum(drive[...] * load, axis=1, keepdims=True)
    diagonal = lax.broadcasted_iota(jnp.int32, (MODE_ROWS, MODES), 0) == lax.broadcasted_iota(
        jnp.int32, (MODE_ROWS, MODES), 1
    )
    amps = [jnp.broadcast_to(amp[m : m + 1], (rows, width)) for m in range(MODES)]
    groups = width // depth
    gains = []
    for t in range(2):
        gain = jnp.zeros((rows, width), F32)
        for m in range(t * groups, min(MODES, (t + 1) * groups)):
            gain = jnp.where(lane // depth == m - t * groups, amps[m], gain)
        gains.append(gain)

    def gather(first, second):
        tile = first * gains[0] + second * gains[1]
        step = depth
        while step < width:
            tile = tile + pltpu.roll(tile, step, 1)
            step *= 2
        return tile

    corner = gather(flux_c[0], flux_c[1])
    columns = {}
    for a, s in enumerate(SIGNS):
        face = gather(flux_y[a, 0], flux_y[a, 1])
        for b, t in enumerate(SIGNS):
            edge = corner[2 * a + b : 2 * a + b + 1]
            moved = pltpu.roll(face, t % rows, 0)
            columns[t, s] = jnp.where(sub == (0 if t == 1 else rows - 1), edge, moved)

    def weigh(terms):
        return tree_sum([amps[m] * terms[m] for m in range(MODES)])

    lines = [
        [
            weigh([flux_x[a, m, r * rows : (r + 1) * rows, :] for m in range(MODES)])
            for r in range(3)
        ]
        for a in range(2)
    ]

    def put(i, z, value):
        stage[i, z] = pre[i, z] + COEF[i] * value

    part = depth // N_CUTS
    for slot in range(depth + 2):
        flux = weigh([flux_m[m, slot] for m in range(MODES)])
        place = LOW if slot == 0 else HIGH if slot == depth + 1 else slot - 1
        for a, s in enumerate(SIGNS):
            line = lines[a][place // rows][place % rows : place % rows + 1]
            moved = pltpu.roll(flux, s % rows, 0)
            moved = jnp.where(sub == (0 if s == 1 else rows - 1), line, moved)
            for i in X_GROUP[a]:
                _, cy, cz = VELOCITY[i]
                z = slot - 1 + cz
                if not 0 <= z < depth:
                    continue
                value = moved
                if cy:
                    value = pltpu.roll(moved, cy % width, 1)
                    column = jnp.broadcast_to(columns[s, cy][:, z : z + 1], (rows, width))
                    value = jnp.where(lane == (0 if cy == 1 else width - 1), column, value)
                put(i, z, value)
        if slot >= 2 and (slot - 1) % part == 0:
            cut = pl.ds(slot - 1 - part, part)
            for first, count in MOVED_RUNS:
                run = pl.ds(first, count)
                write(stage.at[run, cut], out.at[run, cut])
    amplitude[...] = jnp.sum(jnp.where(diagonal, amp, 0.0), axis=0, keepdims=True)
    write(amplitude, amp_out)
    for copy in copies:
        copy.wait()


def per_device(sizes, pops, solid, cell, panel, area, shapes, panel_mode, compliance):
    depth, rows, width = pops.shape[1:]
    n_surf = cell.shape[-1]
    stages = stages_of(sizes)
    n_slots = max(len(stage_offsets(stage, sizes)) + 1 for stage in stages)
    vmem = pl.BlockSpec(memory_space=pltpu.VMEM)
    hbm = pl.BlockSpec(memory_space=pltpu.HBM)
    tile = (rows, width)
    dma = pltpu.SemaphoreType.DMA
    passed = pl.pallas_call(
        functools.partial(exchange, sizes),
        out_shape=(
            jax.ShapeDtypeStruct(pops.shape, F32),
            jax.ShapeDtypeStruct((MODES, depth + 2) + tile, F32),
            jax.ShapeDtypeStruct((2, MODES, depth + rows, width), F32),
            jax.ShapeDtypeStruct((2, 2) + tile, F32),
            jax.ShapeDtypeStruct((2,) + tile, F32),
            jax.ShapeDtypeStruct((1, width), F32),
            jax.ShapeDtypeStruct((MODE_ROWS, PANELS), F32),
        ),
        in_specs=[hbm] * 8,
        out_specs=(vmem,) * 7,
        scratch_shapes=[
            pltpu.VMEM(pops.shape, F32),
            pltpu.VMEM(solid.shape, jnp.int32),
            pltpu.VMEM((1, n_surf), jnp.int32),
            pltpu.VMEM((1, n_surf), jnp.int32),
            pltpu.VMEM((1, n_surf), F32),
            pltpu.VMEM((MODES, 1, n_surf), F32),
            pltpu.VMEM((1, PANELS), jnp.int32),
            pltpu.VMEM((1, MODES), F32),
            pltpu.VMEM((MODE_ROWS, n_surf), F32),
            dma((7 + N_LOADS,)),
            pltpu.VMEM((19, depth + 2) + tile, F32),
            pltpu.VMEM((depth,) + tile, F32),
            pltpu.VMEM((2, 6, depth, 1, width), F32),
            pltpu.VMEM((2, 6, depth + 2, 1, width), F32),
            pltpu.VMEM((2,) + tile, F32),
            pltpu.VMEM((2,) + tile, F32),
            pltpu.VMEM((2, 2) + tile, F32),
            pltpu.VMEM((2, 2) + tile, F32),
            pltpu.VMEM((2, MODE_ROWS, n_surf), F32),
            pltpu.VMEM((2, 2, MODE_ROWS, width), F32),
            pltpu.VMEM((2, 2, MODE_ROWS, width), F32),
            pltpu.VMEM((2, 2) + tile, F32),
            pltpu.VMEM((2, 2) + tile, F32),
            pltpu.VMEM((2, 2, 2, 1, width), F32),
            pltpu.VMEM((2, 2, 2, 1, width), F32),
            dma((N_SURF,)),
            dma((N_SURF,)),
            pltpu.VMEM((len(stages), n_slots, 1, width), F32),
            dma((N_HALO,)),
            dma((N_HALO,)),
            dma((len(stages),)),
            dma((len(stages),)),
        ],
        compiler_params=pltpu.CompilerParams(
            collective_id=0, has_side_effects=True, vmem_limit_bytes=24 * 1024 * 1024
        ),
    )(
        *(
            pltpu.with_memory_space_constraint(x, pltpu.HBM)
            for x in (
                pops,
                solid,
                cell.reshape(1, n_surf),
                panel.reshape(1, n_surf),
                area.reshape(1, n_surf),
                shapes.reshape(MODES, 1, n_surf),
                panel_mode.reshape(1, PANELS),
                compliance.reshape(1, MODES),
            )
        )
    )
    read, force, amp = pl.pallas_call(
        apply,
        out_shape=(
            jax.ShapeDtypeStruct(pops.shape, F32),
            jax.ShapeDtypeStruct((1, PANELS), F32),
            jax.ShapeDtypeStruct((1, MODES), F32),
        ),
        in_specs=[vmem] * 7,
        out_specs=(hbm,) * 3,
        scratch_shapes=[
            pltpu.VMEM(pops.shape, F32),
            pltpu.VMEM((1, PANELS), F32),
            pltpu.VMEM((1, MODES), F32),
            dma((len(FIXED_RUNS) + len(MOVED_RUNS) * N_CUTS + 2,)),
        ],
        compiler_params=pltpu.CompilerParams(vmem_limit_bytes=8 * 1024 * 1024),
    )(*passed)
    return read, force.reshape(PANELS), amp.reshape(MODES)


def solution(mesh):
    placed = (
        P(None, "gz", "gx", "gy"),
        P("gz", "gx", "gy"),
        P("gz", "gx", "gy", None),
        P("gz", "gx", "gy", None),
        P("gz", "gx", "gy", None),
        P("gz", "gx", "gy", None, None),
        P(),
        P(),
    )
    return jax.shard_map(
        functools.partial(per_device, tuple(mesh.shape[a] for a in AXES)),
        mesh=mesh,
        in_specs=placed,
        out_specs=(P(None, "gz", "gx", "gy"), P(), P()),
        check_vma=False,
    )
```

```python
import functools

import jax
import jax.numpy as jnp
from jax import lax
from jax.experimental import pallas as pl
from jax.experimental.pallas import tpu as pltpu
from jax.sharding import PartitionSpec as P

PANELS = 40
MODES = 12
VELOCITY = (
    (0, 0, 0),
    (1, 0, 0),
    (-1, 0, 0),
    (0, 1, 0),
    (0, -1, 0),
    (0, 0, 1),
    (0, 0, -1),
    (1, 1, 0),
    (-1, -1, 0),
    (1, -1, 0),
    (-1, 1, 0),
    (1, 0, 1),
    (-1, 0, -1),
    (1, 0, -1),
    (-1, 0, 1),
    (0, 1, 1),
    (0, -1, -1),
    (0, 1, -1),
    (0, -1, 1),
)
WEIGHTS = (1.0 / 3.0,) + (1.0 / 18.0,) * 6 + (1.0 / 36.0,) * 12
OMEGA = 1.0 / 0.6
WALL_SCALE = 0.02
COEF = tuple(6.0 * w * v[0] for w, v in zip(WEIGHTS, VELOCITY))
SIGNS = (1, -1)


def moving(axis, sign):
    return tuple(i for i in range(19) if VELOCITY[i][axis] == sign)


X_GROUP = tuple(moving(0, s) for s in SIGNS)
Y_GROUP = tuple(moving(1, s) for s in SIGNS)
Z_GROUP = tuple(moving(2, s) for s in SIGNS)
ORDER = Z_GROUP[0] + Z_GROUP[1] + tuple(i for i in range(19) if VELOCITY[i][2] == 0)
PLACE = tuple(ORDER.index(i) for i in range(19))
AXES = ("gx", "gy", "gz")
MESH = pl.DeviceIdType.MESH
N_LOADS = 4
MODE_ROWS = 16
CELL_ROW = MODES
LOW, HIGH = 16, 17
F32 = jnp.float32
BF16 = jnp.bfloat16


def stages_of(sizes):
    if sizes[0] * sizes[1] * sizes[2] <= 64:
        return (AXES,)
    return (("gx",), ("gy", "gz"))


def halves(x):
    high = x.astype(BF16)
    return high, (x - high.astype(F32)).astype(BF16)


def dot(a, b):
    return jnp.dot(a, b, preferred_element_type=F32)


def dot_nt(a, b):
    return lax.dot_general(a, b, (((1,), (1,)), ((), ())), preferred_element_type=F32)


def stage_offsets(stage, sizes):
    result = [(0, 0, 0)]
    for dim, axis in enumerate(AXES):
        if axis in stage:
            result = [
                tuple(k if d == dim else o[d] for d in range(3))
                for o in result
                for k in range(sizes[dim])
            ]
    return [o for o in result if o != (0, 0, 0)]


def offsets_of(sizes):
    found = []
    for i in range(1, 19):
        found.append(tuple(c % n for c, n in zip(VELOCITY[i], sizes)))
    for stage in stages_of(sizes):
        found += stage_offsets(stage, sizes)
    return sorted(set(found))


def tree_sum(terms):
    while len(terms) > 1:
        terms = [sum(terms[k + 1 : k + 2], terms[k]) for k in range(0, len(terms), 2)]
    return terms[0]


N_HALO = 18
PER_DOT = 2
N_SURF = 2 + 4 + 2 + 4 + 2


def exchange(
    sizes,
    pops_in,
    solid_in,
    cell_in,
    panel_in,
    area_in,
    shapes_in,
    panel_mode_in,
    compliance_in,
    pre,
    flux_m,
    flux_x,
    flux_y,
    flux_c,
    column_out,
    total_out,
    drive_out,
    pops,
    solid,
    cell,
    panel,
    area,
    shape_rows,
    panel_mode,
    compliance,
    mine,
    load_sem,
    dens,
    xs,
    xh,
    xe,
    xeh,
    ys,
    yh,
    yr,
    yrh,
    yzh,
    theirs,
    edges,
    edges_in,
    faces,
    faces_in,
    corners,
    corners_in,
    surf_send,
    surf_recv,
    slots,
    send_sem,
    recv_sem,
    stage_send,
    stage_recv,
):
    depth, rows, width = pops.shape[1:]
    cells = depth * rows
    groups = width // depth
    here = tuple(lax.axis_index(a) for a in AXES)
    stages = stages_of(sizes)
    targets = {}

    def at(offset):
        key = tuple(o % n for o, n in zip(offset, sizes))
        if key not in targets:
            targets[key] = tuple(
                lax.rem(h + o, n) if o else h for h, o, n in zip(here, key, sizes)
            )
        return targets[key]

    partners = offsets_of(sizes)
    barrier = pltpu.get_barrier_semaphore()
    for offset in partners:
        pl.semaphore_signal(barrier, inc=1, device_id=at(offset), device_id_type=MESH)

    small = [(cell_in, cell), (panel_in, panel), (area_in, area), (shapes_in, shape_rows)]
    part = depth // N_LOADS
    cuts = [pl.ds(n * part, part) for n in range(N_LOADS)]
    big = [(pops_in.at[:, c], pops.at[:, c]) for c in cuts]
    late = [(solid_in, solid), (panel_mode_in, panel_mode), (compliance_in, compliance)]
    loads = []
    for n, (src, dst) in enumerate(small + big + late):
        loads.append(pltpu.make_async_copy(src, dst, load_sem.at[n]))
        loads[n].start()

    lane = lax.broadcasted_iota(jnp.int32, (rows, width), 1)
    sub = lax.broadcasted_iota(jnp.int32, (rows, width), 0)

    for copy in loads[: len(small)]:
        copy.wait()
    n_surf = cell.shape[1]
    live = panel[...] >= 0
    col = lax.rem(cell[...], width)
    row = lax.div(cell[...], width)
    cell_x = lax.rem(row, rows)
    cell_z = lax.div(row, rows)
    spot = lax.broadcasted_iota(jnp.int32, (width, n_surf), 0)
    pick_col = jnp.where(spot == col, 1.0, 0.0).astype(BF16)
    on_row = lax.broadcasted_iota(jnp.int32, (cells, n_surf), 0) == row

    table = [jnp.where(live, shape_rows[m] * WALL_SCALE, 0.0) for m in range(MODES)]
    table.append(cell[...].astype(F32))
    for m, line in enumerate(table):
        mine[m] = line
    table = jnp.concatenate(
        table[:MODES] + [jnp.zeros((MODE_ROWS - MODES, n_surf), F32)], axis=0
    )
    masked = []
    for a in range(2):
        on_x = cell_x == (rows - 1 if a == 0 else 0)
        for b in range(2):
            on_z = cell_z == (depth - 1 if b == 0 else 0)
            masked.append(jnp.where(on_x & on_z, table, 0.0))
    high, low = halves(jnp.concatenate(masked, axis=0))
    edge_rows = dot_nt(high, pick_col) + dot_nt(low, pick_col)
    for k in range(4):
        edges[k // 2, k % 2] = edge_rows[k * MODE_ROWS : (k + 1) * MODE_ROWS]
    row_id = lax.broadcasted_iota(jnp.int32, (rows, n_surf), 0)
    sides = jnp.concatenate(
        [
            jnp.where((row_id == cell_x) & (col == (width - 1 if a == 0 else 0)), 1.0, 0.0)
            for a in range(2)
        ],
        axis=0,
    ).astype(BF16)
    on_z = lax.rem(spot, depth) == cell_z
    for t in range(2):
        spread_rows = jnp.concatenate(
            [
                jnp.broadcast_to(
                    table[t * groups + g : t * groups + g + 1, :]
                    if t * groups + g < MODES
                    else jnp.zeros((1, n_surf), F32),
                    (depth, n_surf),
                )
                for g in range(groups)
            ],
            axis=0,
        )
        high, low = halves(jnp.where(on_z, spread_rows, 0.0))
        packed = dot_nt(sides, high) + dot_nt(sides, low)
        for a in range(2):
            faces[a, t] = packed[a * rows : (a + 1) * rows]
            for b in range(2):
                edge = a * rows + (rows - 1 if b == 0 else 0)
                corners[a, b, t] = packed[edge : edge + 1]

    def add_up(z, carry):
        density = pops[0, z]
        for i in range(1, 19):
            density = density + pops[i, z]
        dens[pl.ds(pl.multiple_of(z * rows, rows), rows)] = density
        return carry

    for n in range(N_LOADS):
        loads[len(small) + n].wait()
        lax.fori_loop(n * part, (n + 1) * part, add_up, 0, unroll=True)
    gauge_high, gauge_low = halves(dens[...] - 1.0)
    by_row = dot(gauge_high, pick_col) + dot(gauge_low, pick_col)
    excess = jnp.sum(jnp.where(on_row, by_row, 0.0), axis=0, keepdims=True)
    contrib = jnp.where(live, area[...] * (excess / 3.0), 0.0)
    pick_panel = jnp.where(spot == panel[...], 1.0, 0.0).astype(BF16)
    contrib_high, contrib_low = halves(jnp.broadcast_to(contrib, (8, n_surf)))
    partial = dot_nt(contrib_high, pick_panel) + dot_nt(contrib_low, pick_panel)
    partial = partial[0:1]

    pl.semaphore_wait(barrier, len(partners))

    def stage_start(n, value):
        stage = stages[n]
        index = 0
        for dim, axis in enumerate(AXES):
            if axis in stage:
                index = index * sizes[dim] + here[dim]
        slots[n, index] = value
        for offset in stage_offsets(stage, sizes):
            pltpu.make_async_remote_copy(
                src_ref=slots.at[n, index],
                dst_ref=slots.at[n, index],
                send_sem=stage_send.at[n],
                recv_sem=stage_recv.at[n],
                device_id=at(offset),
                device_id_type=MESH,
            ).start()

    def stage_sum(n):
        count = len(stage_offsets(stages[n], sizes))
        whole = pltpu.make_async_remote_copy(
            src_ref=slots.at[n, pl.ds(0, count)],
            dst_ref=slots.at[n, pl.ds(0, count)],
            send_sem=stage_send.at[n],
            recv_sem=stage_recv.at[n],
            device_id=at(stage_offsets(stages[n], sizes)[0]),
            device_id_type=MESH,
        )
        whole.wait_recv()
        whole.wait_send()
        return tree_sum([slots[n, k] for k in range(count + 1)])

    stage_start(0, partial)

    surfels = []

    def pass_on(src, dst, offset):
        copy = pltpu.make_async_remote_copy(
            src_ref=src,
            dst_ref=dst,
            send_sem=surf_send.at[len(surfels)],
            recv_sem=surf_recv.at[len(surfels)],
            device_id=at(offset),
            device_id_type=MESH,
        )
        copy.start()
        surfels.append(copy)

    for a, s in enumerate(SIGNS):
        pass_on(mine, theirs.at[a], (s, 0, 0))
        pass_on(faces.at[a], faces_in.at[a], (0, s, 0))
        for b, t in enumerate(SIGNS):
            pass_on(edges.at[a, b], edges_in.at[a, b], (s, 0, t))
            pass_on(corners.at[a, b], corners_in.at[a, b], (t, s, 0))

    loads[len(small) + N_LOADS].wait()

    def collide(z, packed):
        f = [pops[i, z] for i in range(19)]
        density = dens[pl.ds(pl.multiple_of(z * rows, rows), rows)]
        inverse = 1.0 / density
        u = []
        for axis in range(3):
            plus, minus = moving(axis, 1), moving(axis, -1)
            total = f[plus[0]] - f[minus[0]]
            for i, j in zip(plus[1:], minus[1:]):
                total = total + (f[i] - f[j])
            u.append(total * inverse)
        base = 1.0 - 1.5 * (u[0] * u[0] + u[1] * u[1] + u[2] * u[2])
        fixed = solid[z] == 1
        scaled = [OMEGA * w * density for w in WEIGHTS]
        new = [None] * 19
        new[0] = jnp.where(fixed, f[0], (1.0 - OMEGA) * f[0] + scaled[0] * base)
        for i in range(1, 19, 2):
            proj = None
            for axis in range(3):
                comp = VELOCITY[i][axis]
                if comp:
                    term = u[axis] if comp == 1 else -u[axis]
                    proj = term if proj is None else proj + term
            even = scaled[i] * (base + 4.5 * (proj * proj))
            odd = scaled[i] * (3.0 * proj)
            new[i] = jnp.where(fixed, f[i + 1], (1.0 - OMEGA) * f[i] + (even + odd))
            new[i + 1] = jnp.where(fixed, f[i], (1.0 - OMEGA) * f[i + 1] + (even - odd))
        packed = list(packed)

        def pack(a, value, edge, place):
            column = jnp.broadcast_to(value[:, edge : edge + 1], (rows, width))
            packed[a] = jnp.where(lane == place, column, packed[a])

        for i in range(19):
            cx, cy, cz = VELOCITY[i]
            value = new[i]
            if cx:
                value = pltpu.roll(value, cx % rows, 0)
            if cy:
                value = pltpu.roll(value, cy % width, 1)
                a = SIGNS.index(cy)
                place = z if cz == 0 else lax.rem(z + cz + depth, depth)
                edge = 0 if cy == 1 else width - 1
                pack(a, value, edge, Y_GROUP[a].index(i) * depth + place)
            pre[PLACE[i], pl.ds(pl.multiple_of((z + 1 + cz) * rows, rows), rows)] = value
        for a in range(2):
            pack(a, density, width - 1 if a == 0 else 0, 5 * depth + z)
        return tuple(packed)

    zero = jnp.zeros((rows, width), F32)
    packed = lax.fori_loop(0, depth, collide, (zero, zero))
    line_lane = lax.broadcasted_iota(jnp.int32, (1, width), 1)
    for a in range(2):
        wrap, edge = (0, rows - 1) if a == 0 else (rows - 1, 0)
        for k, i in enumerate(X_GROUP[a]):
            cz = VELOCITY[i][2]
            first = (1 + cz) * rows + wrap
            xs[a, k] = pre[PLACE[i], pl.ds(first, depth, stride=rows), :]
            if cz:
                b = SIGNS.index(cz)
                first = (depth + 1 if b == 0 else 0) * rows + wrap
                xe[a, b, 0] = pre[PLACE[i], first : first + 1, :]
        xs[a, 5] = dens[pl.ds(edge, depth, stride=rows), :]
        for b in range(2):
            first = (depth - 1 if b == 0 else 0) * rows + edge
            xe[a, b, 1] = dens[first : first + 1, :]
            wrap_b, edge_b = (0, rows - 1) if b == 0 else (rows - 1, 0)
            yr[a, b] = jnp.where(
                line_lane < 5 * depth,
                packed[a][wrap_b : wrap_b + 1],
                packed[a][edge_b : edge_b + 1],
            )
        ys[a] = packed[a]

    halo = []

    def send(src, dst, offset):
        copy = pltpu.make_async_remote_copy(
            src_ref=src,
            dst_ref=dst,
            send_sem=send_sem.at[len(halo)],
            recv_sem=recv_sem.at[len(halo)],
            device_id=at(offset),
            device_id_type=MESH,
        )
        copy.start()
        halo.append(copy)

    for a, s in enumerate(SIGNS):
        send(xs.at[a], xh.at[a], (s, 0, 0))
        send(ys.at[a], yh.at[a], (0, s, 0))
        for b, t in enumerate(SIGNS):
            send(yr.at[a, b], yrh.at[a, b], (t, s, 0))
            send(ys.at[a], yzh.at[a, b], (0, s, t))
            send(xe.at[a, b], xeh.at[a, b], (s, 0, t))
        group = pl.ds(a * 5, 5)
        source, target = (depth + 1, 1) if a == 0 else (0, depth)
        send(
            pre.at[group, pl.ds(source * rows, rows)],
            pre.at[group, pl.ds(target * rows, rows)],
            (0, 0, s),
        )

    half = cells // 2
    in_row = lax.broadcasted_iota(jnp.int32, (half, n_surf), 0) == lax.rem(row, half)
    in_row = jnp.where(in_row, 1.0, 0.0).astype(BF16).reshape(half // 16, 16, n_surf)
    wide = lax.broadcasted_iota(jnp.int32, (2 * width, n_surf), 0)
    pick_half = jnp.where(wide == lax.div(row, half) * width + col, 1.0, 0.0).astype(BF16)

    def scatter(step, carry):
        parts = []
        for k in range(PER_DOT):
            line = jnp.broadcast_to(mine[step * PER_DOT + k], (16, n_surf))
            for value in halves(line):
                parts.append((in_row * value[None]).reshape(half, n_surf))
        found = dot_nt(jnp.concatenate(parts, axis=0), pick_half)
        for k in range(PER_DOT):
            first = 2 * k * half
            flux = found[first : first + half] + found[first + half : first + 2 * half]
            for h in range(2):
                value = flux[:, h * width : (h + 1) * width] * dens[h * half : (h + 1) * half]
                value = value.reshape(depth // 2, rows, width)
                flux_m[step * PER_DOT + k, pl.ds(1 + h * (depth // 2), depth // 2)] = value
        return carry

    lax.fori_loop(0, MODES // PER_DOT, scatter, 0)
    for a, s in enumerate(SIGNS):
        source, target = (depth, 0) if a == 0 else (1, depth + 1)
        pass_on(flux_m.at[:, source], flux_m.at[:, target], (0, 0, s))

    for copy in loads[len(small) + N_LOADS + 1 :]:
        copy.wait()
    mode_id = lax.broadcasted_iota(jnp.int32, (MODE_ROWS, PANELS), 0)
    diagonal = lax.broadcasted_iota(jnp.int32, (MODE_ROWS, MODES), 0) == lax.broadcasted_iota(
        jnp.int32, (MODE_ROWS, MODES), 1
    )
    factor = jnp.sum(jnp.where(diagonal, compliance[...], 0.0), axis=1, keepdims=True)
    drive_out[...] = jnp.where(panel_mode[...] == mode_id, factor, 0.0)

    for n in range(1, len(stages)):
        stage_start(n, stage_sum(n - 1))

    for copy in halo:
        copy.wait()

    columns = []
    for a in range(2):
        result = yh[a]
        for j, i in enumerate(Y_GROUP[a]):
            cx, _, cz = VELOCITY[i]
            if cx:
                own = (lane >= j * depth) & (lane < (j + 1) * depth)
                own = own & (sub == (0 if cx == 1 else rows - 1))
                result = jnp.where(own, yrh[a, SIGNS.index(cx)], result)
            if cz:
                place = j * depth if cz == 1 else (j + 1) * depth - 1
                result = jnp.where(lane == place, yzh[a, SIGNS.index(cz)], result)
        columns.append(result)
        column_out[a] = result
    for a in range(2):
        wrap = 0 if a == 0 else rows - 1
        for k, i in enumerate(X_GROUP[a]):
            cz = VELOCITY[i][2]
            pre[PLACE[i], pl.ds((1 + cz) * rows + wrap, depth, stride=rows), :] = xh[a, k]
            if cz:
                first = (1 if cz == 1 else depth) * rows + wrap
                pre[PLACE[i], first : first + 1, :] = xeh[a, SIGNS.index(cz), 0]
    for a in range(2):
        for j, i in enumerate(Y_GROUP[a]):
            if VELOCITY[i][0]:
                continue
            at_edge = lane == (0 if a == 0 else width - 1)
            for z in range(depth):
                tile_rows = pl.ds((z + 1) * rows, rows)
                place = j * depth + z
                column = jnp.broadcast_to(columns[a][:, place : place + 1], (rows, width))
                pre[PLACE[i], tile_rows] = jnp.where(at_edge, column, pre[PLACE[i], tile_rows])

    for copy in surfels:
        copy.wait()

    def everywhere(tile, group):
        tile = jnp.where(lane // depth == group, tile, 0.0)
        step = depth
        while step < width:
            tile = tile + pltpu.roll(tile, step, 1)
            step *= 2
        return tile

    level_id = lax.broadcasted_iota(jnp.int32, (depth, n_surf), 0)
    for a in range(2):
        other = theirs[a, CELL_ROW].astype(jnp.int32)
        pick = jnp.where(spot == lax.rem(other, width), 1.0, 0.0).astype(BF16)
        on_x = lax.rem(lax.div(other, width), rows) == (rows - 1 if a == 0 else 0)
        on_face = (level_id == lax.div(other, width * rows)) & on_x
        lines = jnp.concatenate(
            [jnp.where(on_face, theirs[a, m], 0.0) for m in range(MODES)], axis=0
        )
        high, low = halves(lines)
        lines = dot_nt(high, pick) + dot_nt(low, pick)
        density = xh[a, 5]
        for m in range(MODES):
            flux_x[a, m, 0:depth, :] = lines[m * depth : (m + 1) * depth] * density
        for b in range(2):
            place = LOW if b == 0 else HIGH
            line = xeh[a, b, 1]
            for m in range(MODES):
                flux_x[a, m, place : place + 1, :] = edges_in[a, b, m : m + 1, :] * line
        density = everywhere(yh[a], 5)
        for t in range(2):
            flux_y[a, t] = faces_in[a, t] * density
        for b in range(2):
            density = everywhere(jnp.broadcast_to(yrh[a, b], (rows, width)), 5)
            for t in range(2):
                k = 2 * a + b
                flux_c[t, k : k + 1, :] = corners_in[a, b, t] * density[0:1]
    flux_c[:, 4:, :] = jnp.zeros((2, rows - 4, width), F32)
    for a in range(2):
        for m in range(MODES):
            flux_x[a, m, HIGH + 1 :, :] = jnp.zeros((rows - 2, width), F32)

    total_out[...] = stage_sum(len(stages) - 1)


MOVED = X_GROUP[0] + X_GROUP[1]
FIXED_RUNS = ((0, 1), (3, 2), (5, 1), (6, 1), (15, 1), (16, 1), (17, 1), (18, 1))
MOVED_RUNS = ((1, 2), (7, 8))
N_CUTS = 4


def apply(pre, flux_m, flux_x, flux_y, flux_c, column, total, drive, out, force_out, amp_out, stage, force, amplitude, sem):
    depth, rows, width = flux_m.shape[1] - 2, flux_m.shape[2], flux_m.shape[3]
    copies = []

    def write(src, dst):
        copy = pltpu.make_async_copy(src, dst, sem.at[len(copies)])
        copy.start()
        copies.append(copy)

    for first, count in FIXED_RUNS:
        run = pl.ds(PLACE[first], count)
        write(pre.at[run, pl.ds(rows, depth * rows)], out.at[pl.ds(first, count)])

    lane = lax.broadcasted_iota(jnp.int32, (rows, width), 1)
    sub = lax.broadcasted_iota(jnp.int32, (rows, width), 0)
    load = total[:, :PANELS]
    force[...] = load
    write(force, force_out)
    amp = jnp.sum(drive[...] * load, axis=1, keepdims=True)
    diagonal = lax.broadcasted_iota(jnp.int32, (MODE_ROWS, MODES), 0) == lax.broadcasted_iota(
        jnp.int32, (MODE_ROWS, MODES), 1
    )
    amps = [jnp.broadcast_to(amp[m : m + 1], (rows, width)) for m in range(MODES)]
    groups = width // depth
    gains = []
    for t in range(2):
        gain = jnp.zeros((rows, width), F32)
        for m in range(t * groups, min(MODES, (t + 1) * groups)):
            gain = jnp.where(lane // depth == m - t * groups, amps[m], gain)
        gains.append(gain)

    def gather(first, second):
        tile = first * gains[0] + second * gains[1]
        step = depth
        while step < width:
            tile = tile + pltpu.roll(tile, step, 1)
            step *= 2
        return tile

    corner = gather(flux_c[0], flux_c[1])
    columns = {}
    for a, s in enumerate(SIGNS):
        face = gather(flux_y[a, 0], flux_y[a, 1])
        for b, t in enumerate(SIGNS):
            edge = corner[2 * a + b : 2 * a + b + 1]
            moved = pltpu.roll(face, t % rows, 0)
            moved = jnp.where(sub == (0 if t == 1 else rows - 1), edge, moved)
            i = VELOCITY.index((t, s, 0))
            columns[t, s] = column[a] + COEF[i] * moved

    def weigh(terms):
        return tree_sum([amps[m] * terms[m] for m in range(MODES)])

    lines = [
        [
            weigh([flux_x[a, m, r * rows : (r + 1) * rows, :] for m in range(MODES)])
            for r in range(3)
        ]
        for a in range(2)
    ]

    part = depth // N_CUTS
    for slot in range(depth + 2):
        flux = weigh([flux_m[m, slot] for m in range(MODES)])
        place = LOW if slot == 0 else HIGH if slot == depth + 1 else slot - 1
        for a, s in enumerate(SIGNS):
            line = lines[a][place // rows][place % rows : place % rows + 1]
            moved = pltpu.roll(flux, s % rows, 0)
            moved = jnp.where(sub == (0 if s == 1 else rows - 1), line, moved)
            for i in X_GROUP[a]:
                _, cy, cz = VELOCITY[i]
                z = slot - 1 + cz
                if not 0 <= z < depth:
                    continue
                value = pltpu.roll(moved, cy % width, 1) if cy else moved
                value = pre[PLACE[i], (z + 1) * rows : (z + 2) * rows, :] + COEF[i] * value
                if cy:
                    first = Y_GROUP[SIGNS.index(cy)].index(i) * depth + z
                    beside = columns[s, cy][:, first : first + 1]
                    beside = jnp.broadcast_to(beside, (rows, width))
                    value = jnp.where(lane == (0 if cy == 1 else width - 1), beside, value)
                stage[i, z * rows : (z + 1) * rows] = value
        if slot >= 2 and (slot - 1) % part == 0:
            cut = pl.ds((slot - 1 - part) * rows, part * rows)
            for first, count in MOVED_RUNS:
                run = pl.ds(first, count)
                write(stage.at[run, cut], out.at[run, cut])
    amplitude[...] = jnp.sum(jnp.where(diagonal, amp, 0.0), axis=0, keepdims=True)
    write(amplitude, amp_out)
    for copy in copies:
        copy.wait()


def per_device(sizes, pops, solid, cell, panel, area, shapes, panel_mode, compliance):
    depth, rows, width = pops.shape[1:]
    n_surf = cell.shape[-1]
    stages = stages_of(sizes)
    n_slots = max(len(stage_offsets(stage, sizes)) + 1 for stage in stages)
    vmem = pl.BlockSpec(memory_space=pltpu.VMEM)
    hbm = pl.BlockSpec(memory_space=pltpu.HBM)
    tile = (rows, width)
    dma = pltpu.SemaphoreType.DMA
    passed = pl.pallas_call(
        functools.partial(exchange, sizes),
        out_shape=(
            jax.ShapeDtypeStruct((19, (depth + 2) * rows, width), F32),
            jax.ShapeDtypeStruct((MODES, depth + 2) + tile, F32),
            jax.ShapeDtypeStruct((2, MODES, depth + rows, width), F32),
            jax.ShapeDtypeStruct((2, 2) + tile, F32),
            jax.ShapeDtypeStruct((2,) + tile, F32),
            jax.ShapeDtypeStruct((2,) + tile, F32),
            jax.ShapeDtypeStruct((1, width), F32),
            jax.ShapeDtypeStruct((MODE_ROWS, PANELS), F32),
        ),
        in_specs=[hbm] * 8,
        out_specs=(vmem,) * 8,
        scratch_shapes=[
            pltpu.VMEM(pops.shape, F32),
            pltpu.VMEM(solid.shape, jnp.int32),
            pltpu.VMEM((1, n_surf), jnp.int32),
            pltpu.VMEM((1, n_surf), jnp.int32),
            pltpu.VMEM((1, n_surf), F32),
            pltpu.VMEM((MODES, 1, n_surf), F32),
            pltpu.VMEM((1, PANELS), jnp.int32),
            pltpu.VMEM((1, MODES), F32),
            pltpu.VMEM((MODES + 1, 1, n_surf), F32),
            dma((7 + N_LOADS,)),
            pltpu.VMEM((depth * rows, width), F32),
            pltpu.VMEM((2, 6, depth, width), F32),
            pltpu.VMEM((2, 6, depth, width), F32),
            pltpu.VMEM((2, 2, 2, 1, width), F32),
            pltpu.VMEM((2, 2, 2, 1, width), F32),
            pltpu.VMEM((2,) + tile, F32),
            pltpu.VMEM((2,) + tile, F32),
            pltpu.VMEM((2, 2, 1, width), F32),
            pltpu.VMEM((2, 2, 1, width), F32),
            pltpu.VMEM((2, 2) + tile, F32),
            pltpu.VMEM((2, MODES + 1, 1, n_surf), F32),
            pltpu.VMEM((2, 2, MODE_ROWS, width), F32),
            pltpu.VMEM((2, 2, MODE_ROWS, width), F32),
            pltpu.VMEM((2, 2) + tile, F32),
            pltpu.VMEM((2, 2) + tile, F32),
            pltpu.VMEM((2, 2, 2, 1, width), F32),
            pltpu.VMEM((2, 2, 2, 1, width), F32),
            dma((N_SURF,)),
            dma((N_SURF,)),
            pltpu.VMEM((len(stages), n_slots, 1, width), F32),
            dma((N_HALO,)),
            dma((N_HALO,)),
            dma((len(stages),)),
            dma((len(stages),)),
        ],
        compiler_params=pltpu.CompilerParams(
            collective_id=0, has_side_effects=True, vmem_limit_bytes=24 * 1024 * 1024
        ),
    )(
        *(
            pltpu.with_memory_space_constraint(x, pltpu.HBM)
            for x in (
                pops,
                solid,
                cell.reshape(1, n_surf),
                panel.reshape(1, n_surf),
                area.reshape(1, n_surf),
                shapes.reshape(MODES, 1, n_surf),
                panel_mode.reshape(1, PANELS),
                compliance.reshape(1, MODES),
            )
        )
    )
    read, force, amp = pl.pallas_call(
        apply,
        out_shape=(
            jax.ShapeDtypeStruct((19, depth * rows, width), F32),
            jax.ShapeDtypeStruct((1, PANELS), F32),
            jax.ShapeDtypeStruct((1, MODES), F32),
        ),
        in_specs=[vmem] * 8,
        out_specs=(hbm,) * 3,
        scratch_shapes=[
            pltpu.VMEM((19, depth * rows, width), F32),
            pltpu.VMEM((1, PANELS), F32),
            pltpu.VMEM((1, MODES), F32),
            dma((len(FIXED_RUNS) + len(MOVED_RUNS) * N_CUTS + 2,)),
        ],
        compiler_params=pltpu.CompilerParams(vmem_limit_bytes=8 * 1024 * 1024),
    )(*passed)
    return read.reshape(pops.shape), force.reshape(PANELS), amp.reshape(MODES)


def solution(mesh):
    placed = (
        P(None, "gz", "gx", "gy"),
        P("gz", "gx", "gy"),
        P("gz", "gx", "gy", None),
        P("gz", "gx", "gy", None),
        P("gz", "gx", "gy", None),
        P("gz", "gx", "gy", None, None),
        P(),
        P(),
    )
    return jax.shard_map(
        functools.partial(per_device, tuple(mesh.shape[a] for a in AXES)),
        mesh=mesh,
        in_specs=placed,
        out_specs=(P(None, "gz", "gx", "gy"), P(), P()),
        check_vma=False,
    )
```

```python
import functools

import jax
import jax.numpy as jnp
from jax import lax
from jax.experimental import pallas as pl
from jax.experimental.pallas import tpu as pltpu
from jax.sharding import PartitionSpec as P

PANELS = 40
MODES = 12
VELOCITY = (
    (0, 0, 0),
    (1, 0, 0),
    (-1, 0, 0),
    (0, 1, 0),
    (0, -1, 0),
    (0, 0, 1),
    (0, 0, -1),
    (1, 1, 0),
    (-1, -1, 0),
    (1, -1, 0),
    (-1, 1, 0),
    (1, 0, 1),
    (-1, 0, -1),
    (1, 0, -1),
    (-1, 0, 1),
    (0, 1, 1),
    (0, -1, -1),
    (0, 1, -1),
    (0, -1, 1),
)
WEIGHTS = (1.0 / 3.0,) + (1.0 / 18.0,) * 6 + (1.0 / 36.0,) * 12
OMEGA = 1.0 / 0.6
WALL_SCALE = 0.02
COEF = tuple(6.0 * w * v[0] for w, v in zip(WEIGHTS, VELOCITY))
SIGNS = (1, -1)


def moving(axis, sign):
    return tuple(i for i in range(19) if VELOCITY[i][axis] == sign)


X_GROUP = tuple(moving(0, s) for s in SIGNS)
Y_GROUP = tuple(moving(1, s) for s in SIGNS)
Z_GROUP = tuple(moving(2, s) for s in SIGNS)
ORDER = Z_GROUP[0] + Z_GROUP[1] + tuple(i for i in range(19) if VELOCITY[i][2] == 0)
PLACE = tuple(ORDER.index(i) for i in range(19))
AXES = ("gx", "gy", "gz")
MESH = pl.DeviceIdType.MESH
N_LOADS = 4
MODE_ROWS = 16
CELL_ROW = MODES
LOW, HIGH = 16, 17
F32 = jnp.float32
BF16 = jnp.bfloat16


def stages_of(sizes):
    if sizes[0] * sizes[1] * sizes[2] <= 64:
        return (AXES,)
    return (("gx",), ("gy", "gz"))


def halves(x):
    high = x.astype(BF16)
    return high, (x - high.astype(F32)).astype(BF16)


def dot(a, b):
    return jnp.dot(a, b, preferred_element_type=F32)


def dot_nt(a, b):
    return lax.dot_general(a, b, (((1,), (1,)), ((), ())), preferred_element_type=F32)


def stage_offsets(stage, sizes):
    result = [(0, 0, 0)]
    for dim, axis in enumerate(AXES):
        if axis in stage:
            result = [
                tuple(k if d == dim else o[d] for d in range(3))
                for o in result
                for k in range(sizes[dim])
            ]
    return [o for o in result if o != (0, 0, 0)]


def offsets_of(sizes):
    found = []
    for i in range(1, 19):
        found.append(tuple(c % n for c, n in zip(VELOCITY[i], sizes)))
    for stage in stages_of(sizes):
        found += stage_offsets(stage, sizes)
    return sorted(set(found))


def tree_sum(terms):
    while len(terms) > 1:
        terms = [sum(terms[k + 1 : k + 2], terms[k]) for k in range(0, len(terms), 2)]
    return terms[0]


N_CHUNKS = 2
UNROLL = 4
N_HALO = 16 + 2 * N_CHUNKS
PER_DOT = 2
N_SURF = 2 + 4 + 2 + 4 + 2


def exchange(
    sizes,
    pops_in,
    solid_in,
    cell_in,
    panel_in,
    area_in,
    shapes_in,
    panel_mode_in,
    compliance_in,
    pre,
    flux_m,
    flux_x,
    flux_y,
    flux_c,
    column_out,
    total_out,
    drive_out,
    pops,
    solid,
    cell,
    panel,
    area,
    shape_rows,
    panel_mode,
    compliance,
    mine,
    load_sem,
    dens,
    xs,
    xh,
    xe,
    xeh,
    ys,
    yh,
    yr,
    yrh,
    yzh,
    theirs,
    edges,
    edges_in,
    faces,
    corners,
    corners_in,
    surf_send,
    surf_recv,
    slots,
    send_sem,
    recv_sem,
    stage_send,
    stage_recv,
):
    depth, rows, width = pops.shape[1:]
    cells = depth * rows
    groups = width // depth
    here = tuple(lax.axis_index(a) for a in AXES)
    stages = stages_of(sizes)
    targets = {}

    def at(offset):
        key = tuple(o % n for o, n in zip(offset, sizes))
        if key not in targets:
            targets[key] = tuple(
                lax.rem(h + o, n) if o else h for h, o, n in zip(here, key, sizes)
            )
        return targets[key]

    partners = offsets_of(sizes)
    barrier = pltpu.get_barrier_semaphore()
    for offset in partners:
        pl.semaphore_signal(barrier, inc=1, device_id=at(offset), device_id_type=MESH)

    small = [(cell_in, cell), (panel_in, panel), (area_in, area), (shapes_in, shape_rows)]
    part = depth // N_LOADS
    cuts = [pl.ds(n * part, part) for n in range(N_LOADS)]
    big = [(pops_in.at[:, c], pops.at[:, c]) for c in cuts]
    late = [(solid_in, solid), (panel_mode_in, panel_mode), (compliance_in, compliance)]
    loads = []
    for n, (src, dst) in enumerate(small + big + late):
        loads.append(pltpu.make_async_copy(src, dst, load_sem.at[n]))
        loads[n].start()

    lane = lax.broadcasted_iota(jnp.int32, (rows, width), 1)
    sub = lax.broadcasted_iota(jnp.int32, (rows, width), 0)

    for copy in loads[: len(small)]:
        copy.wait()
    n_surf = cell.shape[1]
    live = panel[...] >= 0
    col = lax.rem(cell[...], width)
    row = lax.div(cell[...], width)
    cell_x = lax.rem(row, rows)
    cell_z = lax.div(row, rows)
    spot = lax.broadcasted_iota(jnp.int32, (width, n_surf), 0)
    pick_col = jnp.where(spot == col, 1.0, 0.0).astype(BF16)
    on_row = lax.broadcasted_iota(jnp.int32, (cells, n_surf), 0) == row

    def add_up(z, carry):
        density = pops[0, z]
        for i in range(1, 19):
            density = density + pops[i, z]
        dens[pl.ds(pl.multiple_of(z * rows, rows), rows)] = density
        return carry

    for n in range(N_LOADS):
        loads[len(small) + n].wait()
        lax.fori_loop(n * part, (n + 1) * part, add_up, 0, unroll=True)
    gauge_high, gauge_low = halves(dens[...] - 1.0)
    by_row = dot(gauge_high, pick_col) + dot(gauge_low, pick_col)
    excess = jnp.sum(jnp.where(on_row, by_row, 0.0), axis=0, keepdims=True)
    contrib = jnp.where(live, area[...] * (excess / 3.0), 0.0)
    pick_panel = jnp.where(spot == panel[...], 1.0, 0.0).astype(BF16)
    contrib_high, contrib_low = halves(jnp.broadcast_to(contrib, (8, n_surf)))
    partial = dot_nt(contrib_high, pick_panel) + dot_nt(contrib_low, pick_panel)
    partial = partial[0:1]

    pl.semaphore_wait(barrier, len(partners))

    def stage_start(n, value):
        stage = stages[n]
        index = 0
        for dim, axis in enumerate(AXES):
            if axis in stage:
                index = index * sizes[dim] + here[dim]
        slots[n, index] = value
        for offset in stage_offsets(stage, sizes):
            pltpu.make_async_remote_copy(
                src_ref=slots.at[n, index],
                dst_ref=slots.at[n, index],
                send_sem=stage_send.at[n],
                recv_sem=stage_recv.at[n],
                device_id=at(offset),
                device_id_type=MESH,
            ).start()

    def stage_sum(n):
        count = len(stage_offsets(stages[n], sizes))
        whole = pltpu.make_async_remote_copy(
            src_ref=slots.at[n, pl.ds(0, count)],
            dst_ref=slots.at[n, pl.ds(0, count)],
            send_sem=stage_send.at[n],
            recv_sem=stage_recv.at[n],
            device_id=at(stage_offsets(stages[n], sizes)[0]),
            device_id_type=MESH,
        )
        whole.wait_recv()
        whole.wait_send()
        return tree_sum([slots[n, k] for k in range(count + 1)])

    stage_start(0, partial)

    surfels = []

    def pass_on(src, dst, offset):
        copy = pltpu.make_async_remote_copy(
            src_ref=src,
            dst_ref=dst,
            send_sem=surf_send.at[len(surfels)],
            recv_sem=surf_recv.at[len(surfels)],
            device_id=at(offset),
            device_id_type=MESH,
        )
        copy.start()
        surfels.append(copy)

    scale = WALL_SCALE * (excess + 1.0)
    table = [jnp.where(live, shape_rows[m] * scale, 0.0) for m in range(MODES)]
    table.append(cell[...].astype(F32))
    for m, line in enumerate(table):
        mine[m] = line
    table = jnp.concatenate(
        table[:MODES] + [jnp.zeros((MODE_ROWS - MODES, n_surf), F32)], axis=0
    )
    for a, s in enumerate(SIGNS):
        pass_on(mine, theirs.at[a], (s, 0, 0))

    row_id = lax.broadcasted_iota(jnp.int32, (rows, n_surf), 0)
    sides = jnp.concatenate(
        [
            jnp.where((row_id == cell_x) & (col == (width - 1 if a == 0 else 0)), 1.0, 0.0)
            for a in range(2)
        ],
        axis=0,
    ).astype(BF16)
    on_z = lax.rem(spot, depth) == cell_z
    for t in range(2):
        spread_rows = jnp.concatenate(
            [
                jnp.broadcast_to(
                    table[t * groups + g : t * groups + g + 1, :]
                    if t * groups + g < MODES
                    else jnp.zeros((1, n_surf), F32),
                    (depth, n_surf),
                )
                for g in range(groups)
            ],
            axis=0,
        )
        high, low = halves(jnp.where(on_z, spread_rows, 0.0))
        packed = dot_nt(sides, high) + dot_nt(sides, low)
        for a in range(2):
            faces[a, t] = packed[a * rows : (a + 1) * rows]
            for b in range(2):
                edge = a * rows + (rows - 1 if b == 0 else 0)
                corners[a, b, t] = packed[edge : edge + 1]

    for a, s in enumerate(SIGNS):
        pass_on(faces.at[a], flux_y.at[a], (0, s, 0))
        for b, t in enumerate(SIGNS):
            pass_on(corners.at[a, b], corners_in.at[a, b], (t, s, 0))

    loads[len(small) + N_LOADS].wait()

    def collide(z, packed):
        f = [pops[i, z] for i in range(19)]
        density = dens[pl.ds(pl.multiple_of(z * rows, rows), rows)]
        inverse = 1.0 / density
        u = []
        for axis in range(3):
            plus, minus = moving(axis, 1), moving(axis, -1)
            total = f[plus[0]] - f[minus[0]]
            for i, j in zip(plus[1:], minus[1:]):
                total = total + (f[i] - f[j])
            u.append(total * inverse)
        base = 1.0 - 1.5 * (u[0] * u[0] + u[1] * u[1] + u[2] * u[2])
        fixed = solid[z] == 1
        scaled = [OMEGA * w * density for w in WEIGHTS]
        new = [None] * 19
        new[0] = jnp.where(fixed, f[0], (1.0 - OMEGA) * f[0] + scaled[0] * base)
        for i in range(1, 19, 2):
            proj = None
            for axis in range(3):
                comp = VELOCITY[i][axis]
                if comp:
                    term = u[axis] if comp == 1 else -u[axis]
                    proj = term if proj is None else proj + term
            even = scaled[i] * (base + 4.5 * (proj * proj))
            odd = scaled[i] * (3.0 * proj)
            new[i] = jnp.where(fixed, f[i + 1], (1.0 - OMEGA) * f[i] + (even + odd))
            new[i + 1] = jnp.where(fixed, f[i], (1.0 - OMEGA) * f[i + 1] + (even - odd))
        packed = list(packed)

        def pack(a, value, edge, place):
            column = jnp.broadcast_to(value[:, edge : edge + 1], (rows, width))
            packed[a] = jnp.where(lane == place, column, packed[a])

        for i in range(19):
            cx, cy, cz = VELOCITY[i]
            value = new[i]
            if cx:
                value = pltpu.roll(value, cx % rows, 0)
            if cy:
                value = pltpu.roll(value, cy % width, 1)
                a = SIGNS.index(cy)
                place = z if cz == 0 else lax.rem(z + cz + depth, depth)
                edge = 0 if cy == 1 else width - 1
                pack(a, value, edge, Y_GROUP[a].index(i) * depth + place)
            pre[PLACE[i], pl.ds(pl.multiple_of((z + 1 + cz) * rows, rows), rows)] = value
        return tuple(packed)

    halo = []

    def send(src, dst, offset):
        copy = pltpu.make_async_remote_copy(
            src_ref=src,
            dst_ref=dst,
            send_sem=send_sem.at[len(halo)],
            recv_sem=recv_sem.at[len(halo)],
            device_id=at(offset),
            device_id_type=MESH,
        )
        copy.start()
        halo.append(copy)

    zero = jnp.zeros((rows, width), F32)
    packed = (zero, zero)
    chunk = depth // N_CHUNKS
    for n in range(N_CHUNKS):
        packed = lax.fori_loop(n * chunk, (n + 1) * chunk, collide, packed, unroll=UNROLL)
        for a, s in enumerate(SIGNS):
            wrap = 0 if a == 0 else rows - 1
            for k, i in enumerate(X_GROUP[a]):
                first = (n * chunk + 1 + VELOCITY[i][2]) * rows + wrap
                xs[a, n, k] = pre[PLACE[i], pl.ds(first, chunk, stride=rows), :]
            send(xs.at[a, n], xh.at[a, n], (s, 0, 0))
    for a in range(2):
        wrap = 0 if a == 0 else rows - 1
        for k, i in enumerate(X_GROUP[a]):
            cz = VELOCITY[i][2]
            if cz:
                b = SIGNS.index(cz)
                first = (depth + 1 if b == 0 else 0) * rows + wrap
                xe[a, b] = pre[PLACE[i], first : first + 1, :]
        for b in range(2):
            wrap = 0 if b == 0 else rows - 1
            yr[a, b] = packed[a][wrap : wrap + 1]
        ys[a] = packed[a]

    for a, s in enumerate(SIGNS):
        send(ys.at[a], yh.at[a], (0, s, 0))
        for b, t in enumerate(SIGNS):
            send(yr.at[a, b], yrh.at[a, b], (t, s, 0))
            send(ys.at[a], yzh.at[a, b], (0, s, t))
            send(xe.at[a, b], xeh.at[a, b], (s, 0, t))
        group = pl.ds(a * 5, 5)
        source, target = (depth + 1, 1) if a == 0 else (0, depth)
        send(
            pre.at[group, pl.ds(source * rows, rows)],
            pre.at[group, pl.ds(target * rows, rows)],
            (0, 0, s),
        )

    half = cells // 2
    in_row = lax.broadcasted_iota(jnp.int32, (half, n_surf), 0) == lax.rem(row, half)
    in_row = jnp.where(in_row, 1.0, 0.0).astype(BF16).reshape(half // 16, 16, n_surf)
    wide = lax.broadcasted_iota(jnp.int32, (2 * width, n_surf), 0)
    pick_half = jnp.where(wide == lax.div(row, half) * width + col, 1.0, 0.0).astype(BF16)

    def scatter(step, carry):
        parts = []
        for k in range(PER_DOT):
            line = jnp.broadcast_to(mine[step * PER_DOT + k], (16, n_surf))
            for value in halves(line):
                parts.append((in_row * value[None]).reshape(half, n_surf))
        found = dot_nt(jnp.concatenate(parts, axis=0), pick_half)
        for k in range(PER_DOT):
            first = 2 * k * half
            flux = found[first : first + half] + found[first + half : first + 2 * half]
            for h in range(2):
                value = flux[:, h * width : (h + 1) * width].reshape(depth // 2, rows, width)
                flux_m[step * PER_DOT + k, pl.ds(1 + h * (depth // 2), depth // 2)] = value
        return carry

    lax.fori_loop(0, MODES // PER_DOT, scatter, 0, unroll=True)
    for a, s in enumerate(SIGNS):
        source, target = (depth, 0) if a == 0 else (1, depth + 1)
        pass_on(flux_m.at[:, source], flux_m.at[:, target], (0, 0, s))

    for copy in loads[len(small) + N_LOADS + 1 :]:
        copy.wait()
    mode_id = lax.broadcasted_iota(jnp.int32, (MODE_ROWS, PANELS), 0)
    diagonal = lax.broadcasted_iota(jnp.int32, (MODE_ROWS, MODES), 0) == lax.broadcasted_iota(
        jnp.int32, (MODE_ROWS, MODES), 1
    )
    factor = jnp.sum(jnp.where(diagonal, compliance[...], 0.0), axis=1, keepdims=True)
    drive_out[...] = jnp.where(panel_mode[...] == mode_id, factor, 0.0)

    for n in range(1, len(stages)):
        stage_start(n, stage_sum(n - 1))

    for copy in surfels[:-2]:
        copy.wait()
    late = len(surfels) - 2
    level_id = lax.broadcasted_iota(jnp.int32, (depth, n_surf), 0)
    for a in range(2):
        other = theirs[a, CELL_ROW].astype(jnp.int32)
        pick = jnp.where(spot == lax.rem(other, width), 1.0, 0.0).astype(BF16)
        on_x = lax.rem(lax.div(other, width), rows) == (rows - 1 if a == 0 else 0)
        on_face = (level_id == lax.div(other, width * rows)) & on_x
        lines = jnp.concatenate(
            [jnp.where(on_face, theirs[a, m], 0.0) for m in range(MODES)], axis=0
        )
        high, low = halves(lines)
        lines = dot_nt(high, pick) + dot_nt(low, pick)
        for m in range(MODES):
            flux_x[a, m, 0:depth, :] = lines[m * depth : (m + 1) * depth]
            flux_x[a, m, HIGH + 1 :, :] = jnp.zeros((rows - 2, width), F32)
            for b in range(2):
                first = m * depth + (depth - 1 if b == 0 else 0)
                edges[a, b, m : m + 1, :] = lines[first : first + 1]
        for b, t in enumerate(SIGNS):
            edges[a, b, MODES:, :] = jnp.zeros((MODE_ROWS - MODES, width), F32)
            pass_on(edges.at[a, b], edges_in.at[a, b], (0, 0, t))
            for t in range(2):
                k = 2 * a + b
                flux_c[t, k : k + 1, :] = corners_in[a, b, t]
    flux_c[:, 4:, :] = jnp.zeros((2, rows - 4, width), F32)

    for copy in halo:
        copy.wait()

    columns = []
    for a in range(2):
        result = yh[a]
        for j, i in enumerate(Y_GROUP[a]):
            cx, _, cz = VELOCITY[i]
            if cx:
                own = (lane >= j * depth) & (lane < (j + 1) * depth)
                own = own & (sub == (0 if cx == 1 else rows - 1))
                result = jnp.where(own, yrh[a, SIGNS.index(cx)], result)
            if cz:
                place = j * depth if cz == 1 else (j + 1) * depth - 1
                result = jnp.where(lane == place, yzh[a, SIGNS.index(cz)], result)
        columns.append(result)
        column_out[a] = result
    for a in range(2):
        wrap = 0 if a == 0 else rows - 1
        for k, i in enumerate(X_GROUP[a]):
            cz = VELOCITY[i][2]
            for n in range(N_CHUNKS):
                first = (n * chunk + 1 + cz) * rows + wrap
                pre[PLACE[i], pl.ds(first, chunk, stride=rows), :] = xh[a, n, k]
            if cz:
                first = (1 if cz == 1 else depth) * rows + wrap
                pre[PLACE[i], first : first + 1, :] = xeh[a, SIGNS.index(cz)]
    for a in range(2):
        for j, i in enumerate(Y_GROUP[a]):
            if VELOCITY[i][0]:
                continue
            at_edge = lane == (0 if a == 0 else width - 1)
            for z in range(depth):
                tile_rows = pl.ds((z + 1) * rows, rows)
                place = j * depth + z
                column = jnp.broadcast_to(columns[a][:, place : place + 1], (rows, width))
                pre[PLACE[i], tile_rows] = jnp.where(at_edge, column, pre[PLACE[i], tile_rows])


    for copy in surfels[late:]:
        copy.wait()
    for a in range(2):
        for b in range(2):
            place = LOW if b == 0 else HIGH
            for m in range(MODES):
                flux_x[a, m, place : place + 1, :] = edges_in[a, b, m : m + 1, :]

    total_out[...] = stage_sum(len(stages) - 1)


MOVED = X_GROUP[0] + X_GROUP[1]
FIXED_RUNS = ((0, 1), (3, 2), (5, 1), (6, 1), (15, 1), (16, 1), (17, 1), (18, 1))
MOVED_RUNS = ((1, 2), (7, 8))
N_CUTS = 4


def apply(pre, flux_m, flux_x, flux_y, flux_c, column, total, drive, out, force_out, amp_out, stage, force, amplitude, sem):
    depth, rows, width = flux_m.shape[1] - 2, flux_m.shape[2], flux_m.shape[3]
    copies = []

    def write(src, dst):
        copy = pltpu.make_async_copy(src, dst, sem.at[len(copies)])
        copy.start()
        copies.append(copy)

    for first, count in FIXED_RUNS:
        run = pl.ds(PLACE[first], count)
        write(pre.at[run, pl.ds(rows, depth * rows)], out.at[pl.ds(first, count)])

    lane = lax.broadcasted_iota(jnp.int32, (rows, width), 1)
    sub = lax.broadcasted_iota(jnp.int32, (rows, width), 0)
    load = total[:, :PANELS]
    force[...] = load
    write(force, force_out)
    amp = jnp.sum(drive[...] * load, axis=1, keepdims=True)
    diagonal = lax.broadcasted_iota(jnp.int32, (MODE_ROWS, MODES), 0) == lax.broadcasted_iota(
        jnp.int32, (MODE_ROWS, MODES), 1
    )
    amps = [jnp.broadcast_to(amp[m : m + 1], (rows, width)) for m in range(MODES)]
    groups = width // depth
    gains = []
    for t in range(2):
        gain = jnp.zeros((rows, width), F32)
        for m in range(t * groups, min(MODES, (t + 1) * groups)):
            gain = jnp.where(lane // depth == m - t * groups, amps[m], gain)
        gains.append(gain)

    def gather(first, second):
        tile = first * gains[0] + second * gains[1]
        step = depth
        while step < width:
            tile = tile + pltpu.roll(tile, step, 1)
            step *= 2
        return tile

    corner = gather(flux_c[0], flux_c[1])
    columns = {}
    for a, s in enumerate(SIGNS):
        face = gather(flux_y[a, 0], flux_y[a, 1])
        for b, t in enumerate(SIGNS):
            edge = corner[2 * a + b : 2 * a + b + 1]
            moved = pltpu.roll(face, t % rows, 0)
            moved = jnp.where(sub == (0 if t == 1 else rows - 1), edge, moved)
            i = VELOCITY.index((t, s, 0))
            columns[t, s] = column[a] + COEF[i] * moved

    def weigh(terms):
        return tree_sum([amps[m] * terms[m] for m in range(MODES)])

    lines = [
        [
            weigh([flux_x[a, m, r * rows : (r + 1) * rows, :] for m in range(MODES)])
            for r in range(3)
        ]
        for a in range(2)
    ]

    part = depth // N_CUTS
    for slot in range(depth + 2):
        flux = weigh([flux_m[m, slot] for m in range(MODES)])
        place = LOW if slot == 0 else HIGH if slot == depth + 1 else slot - 1
        for a, s in enumerate(SIGNS):
            line = lines[a][place // rows][place % rows : place % rows + 1]
            moved = pltpu.roll(flux, s % rows, 0)
            moved = jnp.where(sub == (0 if s == 1 else rows - 1), line, moved)
            for i in X_GROUP[a]:
                _, cy, cz = VELOCITY[i]
                z = slot - 1 + cz
                if not 0 <= z < depth:
                    continue
                value = pltpu.roll(moved, cy % width, 1) if cy else moved
                value = pre[PLACE[i], (z + 1) * rows : (z + 2) * rows, :] + COEF[i] * value
                if cy:
                    first = Y_GROUP[SIGNS.index(cy)].index(i) * depth + z
                    beside = columns[s, cy][:, first : first + 1]
                    beside = jnp.broadcast_to(beside, (rows, width))
                    value = jnp.where(lane == (0 if cy == 1 else width - 1), beside, value)
                stage[i, z * rows : (z + 1) * rows] = value
        if slot >= 2 and (slot - 1) % part == 0:
            cut = pl.ds((slot - 1 - part) * rows, part * rows)
            for first, count in MOVED_RUNS:
                run = pl.ds(first, count)
                write(stage.at[run, cut], out.at[run, cut])
    amplitude[...] = jnp.sum(jnp.where(diagonal, amp, 0.0), axis=0, keepdims=True)
    write(amplitude, amp_out)
    for copy in copies:
        copy.wait()


def per_device(sizes, pops, solid, cell, panel, area, shapes, panel_mode, compliance):
    depth, rows, width = pops.shape[1:]
    n_surf = cell.shape[-1]
    stages = stages_of(sizes)
    n_slots = max(len(stage_offsets(stage, sizes)) + 1 for stage in stages)
    vmem = pl.BlockSpec(memory_space=pltpu.VMEM)
    hbm = pl.BlockSpec(memory_space=pltpu.HBM)
    tile = (rows, width)
    dma = pltpu.SemaphoreType.DMA
    passed = pl.pallas_call(
        functools.partial(exchange, sizes),
        out_shape=(
            jax.ShapeDtypeStruct((19, (depth + 2) * rows, width), F32),
            jax.ShapeDtypeStruct((MODES, depth + 2) + tile, F32),
            jax.ShapeDtypeStruct((2, MODES, depth + rows, width), F32),
            jax.ShapeDtypeStruct((2, 2) + tile, F32),
            jax.ShapeDtypeStruct((2,) + tile, F32),
            jax.ShapeDtypeStruct((2,) + tile, F32),
            jax.ShapeDtypeStruct((1, width), F32),
            jax.ShapeDtypeStruct((MODE_ROWS, PANELS), F32),
        ),
        in_specs=[hbm] * 8,
        out_specs=(vmem,) * 8,
        scratch_shapes=[
            pltpu.VMEM(pops.shape, F32),
            pltpu.VMEM(solid.shape, jnp.int32),
            pltpu.VMEM((1, n_surf), jnp.int32),
            pltpu.VMEM((1, n_surf), jnp.int32),
            pltpu.VMEM((1, n_surf), F32),
            pltpu.VMEM((MODES, 1, n_surf), F32),
            pltpu.VMEM((1, PANELS), jnp.int32),
            pltpu.VMEM((1, MODES), F32),
            pltpu.VMEM((MODES + 1, 1, n_surf), F32),
            dma((7 + N_LOADS,)),
            pltpu.VMEM((depth * rows, width), F32),
            pltpu.VMEM((2, N_CHUNKS, 5, depth // N_CHUNKS, width), F32),
            pltpu.VMEM((2, N_CHUNKS, 5, depth // N_CHUNKS, width), F32),
            pltpu.VMEM((2, 2, 1, width), F32),
            pltpu.VMEM((2, 2, 1, width), F32),
            pltpu.VMEM((2,) + tile, F32),
            pltpu.VMEM((2,) + tile, F32),
            pltpu.VMEM((2, 2, 1, width), F32),
            pltpu.VMEM((2, 2, 1, width), F32),
            pltpu.VMEM((2, 2) + tile, F32),
            pltpu.VMEM((2, MODES + 1, 1, n_surf), F32),
            pltpu.VMEM((2, 2, MODE_ROWS, width), F32),
            pltpu.VMEM((2, 2, MODE_ROWS, width), F32),
            pltpu.VMEM((2, 2) + tile, F32),
            pltpu.VMEM((2, 2, 2, 1, width), F32),
            pltpu.VMEM((2, 2, 2, 1, width), F32),
            dma((N_SURF,)),
            dma((N_SURF,)),
            pltpu.VMEM((len(stages), n_slots, 1, width), F32),
            dma((N_HALO,)),
            dma((N_HALO,)),
            dma((len(stages),)),
            dma((len(stages),)),
        ],
        compiler_params=pltpu.CompilerParams(
            collective_id=0, has_side_effects=True, vmem_limit_bytes=24 * 1024 * 1024
        ),
    )(
        *(
            pltpu.with_memory_space_constraint(x, pltpu.HBM)
            for x in (
                pops,
                solid,
                cell.reshape(1, n_surf),
                panel.reshape(1, n_surf),
                area.reshape(1, n_surf),
                shapes.reshape(MODES, 1, n_surf),
                panel_mode.reshape(1, PANELS),
                compliance.reshape(1, MODES),
            )
        )
    )
    read, force, amp = pl.pallas_call(
        apply,
        out_shape=(
            jax.ShapeDtypeStruct((19, depth * rows, width), F32),
            jax.ShapeDtypeStruct((1, PANELS), F32),
            jax.ShapeDtypeStruct((1, MODES), F32),
        ),
        in_specs=[vmem] * 8,
        out_specs=(hbm,) * 3,
        scratch_shapes=[
            pltpu.VMEM((19, depth * rows, width), F32),
            pltpu.VMEM((1, PANELS), F32),
            pltpu.VMEM((1, MODES), F32),
            dma((len(FIXED_RUNS) + len(MOVED_RUNS) * N_CUTS + 2,)),
        ],
        compiler_params=pltpu.CompilerParams(vmem_limit_bytes=8 * 1024 * 1024),
    )(*passed)
    return read.reshape(pops.shape), force.reshape(PANELS), amp.reshape(MODES)


def solution(mesh):
    placed = (
        P(None, "gz", "gx", "gy"),
        P("gz", "gx", "gy"),
        P("gz", "gx", "gy", None),
        P("gz", "gx", "gy", None),
        P("gz", "gx", "gy", None),
        P("gz", "gx", "gy", None, None),
        P(),
        P(),
    )
    return jax.shard_map(
        functools.partial(per_device, tuple(mesh.shape[a] for a in AXES)),
        mesh=mesh,
        in_specs=placed,
        out_specs=(P(None, "gz", "gx", "gy"), P(), P()),
        check_vma=False,
    )
```

```python
import functools

import jax
import jax.numpy as jnp
from jax import lax
from jax.experimental import pallas as pl
from jax.experimental.pallas import tpu as pltpu
from jax.sharding import PartitionSpec as P

PANELS = 40
MODES = 12
VELOCITY = (
    (0, 0, 0),
    (1, 0, 0),
    (-1, 0, 0),
    (0, 1, 0),
    (0, -1, 0),
    (0, 0, 1),
    (0, 0, -1),
    (1, 1, 0),
    (-1, -1, 0),
    (1, -1, 0),
    (-1, 1, 0),
    (1, 0, 1),
    (-1, 0, -1),
    (1, 0, -1),
    (-1, 0, 1),
    (0, 1, 1),
    (0, -1, -1),
    (0, 1, -1),
    (0, -1, 1),
)
WEIGHTS = (1.0 / 3.0,) + (1.0 / 18.0,) * 6 + (1.0 / 36.0,) * 12
OMEGA = 1.0 / 0.6
WALL_SCALE = 0.02
COEF = tuple(6.0 * w * v[0] for w, v in zip(WEIGHTS, VELOCITY))
SIGNS = (1, -1)


def moving(axis, sign):
    return tuple(i for i in range(19) if VELOCITY[i][axis] == sign)


X_GROUP = tuple(moving(0, s) for s in SIGNS)
Y_GROUP = tuple(moving(1, s) for s in SIGNS)
Z_GROUP = tuple(moving(2, s) for s in SIGNS)
ORDER = Z_GROUP[0] + Z_GROUP[1] + tuple(i for i in range(19) if VELOCITY[i][2] == 0)
PLACE = tuple(ORDER.index(i) for i in range(19))
AXES = ("gx", "gy", "gz")
MESH = pl.DeviceIdType.MESH
N_LOADS = 4
MODE_ROWS = 16
CELL_ROW = MODES
LOW, HIGH = 16, 17
F32 = jnp.float32
BF16 = jnp.bfloat16


def stages_of(sizes):
    if sizes[0] * sizes[1] * sizes[2] <= 64:
        return (AXES,)
    return (("gx",), ("gy", "gz"))


def halves(x):
    high = x.astype(BF16)
    return high, (x - high.astype(F32)).astype(BF16)


def dot(a, b):
    return jnp.dot(a, b, preferred_element_type=F32)


def dot_nt(a, b):
    return lax.dot_general(a, b, (((1,), (1,)), ((), ())), preferred_element_type=F32)


def stage_offsets(stage, sizes):
    result = [(0, 0, 0)]
    for dim, axis in enumerate(AXES):
        if axis in stage:
            result = [
                tuple(k if d == dim else o[d] for d in range(3))
                for o in result
                for k in range(sizes[dim])
            ]
    return [o for o in result if o != (0, 0, 0)]


def offsets_of(sizes):
    found = []
    for i in range(1, 19):
        found.append(tuple(c % n for c, n in zip(VELOCITY[i], sizes)))
    for stage in stages_of(sizes):
        found += stage_offsets(stage, sizes)
    return sorted(set(found))


def tree_sum(terms):
    while len(terms) > 1:
        terms = [sum(terms[k + 1 : k + 2], terms[k]) for k in range(0, len(terms), 2)]
    return terms[0]


UNROLL = 4
N_HALO = 18
PER_DOT = 2
N_SURF = 2 + 4 + 2 + 4 + 2


def exchange(
    sizes,
    pops_in,
    solid_in,
    cell_in,
    panel_in,
    area_in,
    shapes_in,
    panel_mode_in,
    compliance_in,
    pre,
    flux_m,
    flux_x,
    flux_y,
    flux_c,
    column_out,
    total_out,
    drive_out,
    pops,
    solid,
    cell,
    panel,
    area,
    shape_rows,
    panel_mode,
    compliance,
    mine,
    load_sem,
    post,
    dens,
    xs,
    xh,
    xe,
    xeh,
    ys,
    yh,
    yr,
    yrh,
    yzh,
    theirs,
    edges,
    edges_in,
    faces,
    corners,
    corners_in,
    surf_send,
    surf_recv,
    slots,
    send_sem,
    recv_sem,
    stage_send,
    stage_recv,
):
    depth, rows, width = pops.shape[1:]
    cells = depth * rows
    groups = width // depth
    here = tuple(lax.axis_index(a) for a in AXES)
    stages = stages_of(sizes)
    targets = {}

    def at(offset):
        key = tuple(o % n for o, n in zip(offset, sizes))
        if key not in targets:
            targets[key] = tuple(
                lax.rem(h + o, n) if o else h for h, o, n in zip(here, key, sizes)
            )
        return targets[key]

    partners = offsets_of(sizes)
    barrier = pltpu.get_barrier_semaphore()
    for offset in partners:
        pl.semaphore_signal(barrier, inc=1, device_id=at(offset), device_id_type=MESH)

    small = [(cell_in, cell), (panel_in, panel), (area_in, area), (shapes_in, shape_rows)]
    part = depth // N_LOADS
    cuts = [pl.ds(n * part, part) for n in range(N_LOADS)]
    big = [(pops_in.at[:, c], pops.at[:, c]) for c in cuts]
    late = [(solid_in, solid), (panel_mode_in, panel_mode), (compliance_in, compliance)]
    loads = []
    for n, (src, dst) in enumerate(small + big + late):
        loads.append(pltpu.make_async_copy(src, dst, load_sem.at[n]))
        loads[n].start()

    lane = lax.broadcasted_iota(jnp.int32, (rows, width), 1)
    sub = lax.broadcasted_iota(jnp.int32, (rows, width), 0)

    for copy in loads[: len(small)]:
        copy.wait()
    n_surf = cell.shape[1]
    live = panel[...] >= 0
    col = lax.rem(cell[...], width)
    row = lax.div(cell[...], width)
    cell_x = lax.rem(row, rows)
    cell_z = lax.div(row, rows)
    spot = lax.broadcasted_iota(jnp.int32, (width, n_surf), 0)
    pick_col = jnp.where(spot == col, 1.0, 0.0).astype(BF16)
    on_row = lax.broadcasted_iota(jnp.int32, (cells, n_surf), 0) == row

    def add_up(z, carry):
        density = pops[0, z]
        for i in range(1, 19):
            density = density + pops[i, z]
        dens[pl.ds(pl.multiple_of(z * rows, rows), rows)] = density
        return carry

    for n in range(N_LOADS):
        loads[len(small) + n].wait()
        lax.fori_loop(n * part, (n + 1) * part, add_up, 0, unroll=True)
    def stage_start(n, value):
        stage = stages[n]
        index = 0
        for dim, axis in enumerate(AXES):
            if axis in stage:
                index = index * sizes[dim] + here[dim]
        slots[n, index] = value
        for offset in stage_offsets(stage, sizes):
            pltpu.make_async_remote_copy(
                src_ref=slots.at[n, index],
                dst_ref=slots.at[n, index],
                send_sem=stage_send.at[n],
                recv_sem=stage_recv.at[n],
                device_id=at(offset),
                device_id_type=MESH,
            ).start()

    def stage_sum(n):
        count = len(stage_offsets(stages[n], sizes))
        whole = pltpu.make_async_remote_copy(
            src_ref=slots.at[n, pl.ds(0, count)],
            dst_ref=slots.at[n, pl.ds(0, count)],
            send_sem=stage_send.at[n],
            recv_sem=stage_recv.at[n],
            device_id=at(stage_offsets(stages[n], sizes)[0]),
            device_id_type=MESH,
        )
        whole.wait_recv()
        whole.wait_send()
        return tree_sum([slots[n, k] for k in range(count + 1)])

    surfels = []

    def pass_on(src, dst, offset):
        copy = pltpu.make_async_remote_copy(
            src_ref=src,
            dst_ref=dst,
            send_sem=surf_send.at[len(surfels)],
            recv_sem=surf_recv.at[len(surfels)],
            device_id=at(offset),
            device_id_type=MESH,
        )
        copy.start()
        surfels.append(copy)

    gauge_high, gauge_low = halves(dens[...] - 1.0)
    by_row = dot(gauge_high, pick_col) + dot(gauge_low, pick_col)
    excess = jnp.sum(jnp.where(on_row, by_row, 0.0), axis=0, keepdims=True)
    contrib = jnp.where(live, area[...] * (excess / 3.0), 0.0)
    pick_panel = jnp.where(spot == panel[...], 1.0, 0.0).astype(BF16)
    contrib_high, contrib_low = halves(jnp.broadcast_to(contrib, (8, n_surf)))
    partial = dot_nt(contrib_high, pick_panel) + dot_nt(contrib_low, pick_panel)
    partial = partial[0:1]


    scale = WALL_SCALE * (excess + 1.0)
    table = [jnp.where(live, shape_rows[m] * scale, 0.0) for m in range(MODES)]
    table.append(cell[...].astype(F32))
    for m, line in enumerate(table):
        mine[m] = line
    table = jnp.concatenate(
        table[:MODES] + [jnp.zeros((MODE_ROWS - MODES, n_surf), F32)], axis=0
    )

    pl.semaphore_wait(barrier, len(partners))


    for a, s in enumerate(SIGNS):
        pass_on(mine, theirs.at[a], (s, 0, 0))


    stage_start(0, partial)


    loads[len(small) + N_LOADS].wait()

    def collide(z, packed):
        f = [pops[i, z] for i in range(19)]
        density = dens[pl.ds(pl.multiple_of(z * rows, rows), rows)]
        inverse = 1.0 / density
        u = []
        for axis in range(3):
            plus, minus = moving(axis, 1), moving(axis, -1)
            total = f[plus[0]] - f[minus[0]]
            for i, j in zip(plus[1:], minus[1:]):
                total = total + (f[i] - f[j])
            u.append(total * inverse)
        base = 1.0 - 1.5 * (u[0] * u[0] + u[1] * u[1] + u[2] * u[2])
        fixed = solid[z] == 1
        scaled = [OMEGA * w * density for w in WEIGHTS]
        new = [None] * 19
        new[0] = jnp.where(fixed, f[0], (1.0 - OMEGA) * f[0] + scaled[0] * base)
        for i in range(1, 19, 2):
            proj = None
            for axis in range(3):
                comp = VELOCITY[i][axis]
                if comp:
                    term = u[axis] if comp == 1 else -u[axis]
                    proj = term if proj is None else proj + term
            even = scaled[i] * (base + 4.5 * (proj * proj))
            odd = scaled[i] * (3.0 * proj)
            new[i] = jnp.where(fixed, f[i + 1], (1.0 - OMEGA) * f[i] + (even + odd))
            new[i + 1] = jnp.where(fixed, f[i], (1.0 - OMEGA) * f[i + 1] + (even - odd))
        packed = list(packed)

        def pack(a, value, edge, place):
            column = jnp.broadcast_to(value[:, edge : edge + 1], (rows, width))
            packed[a] = jnp.where(lane == place, column, packed[a])

        for i in range(19):
            cx, cy, cz = VELOCITY[i]
            if cx or cy:
                post[PLACE[i], pl.ds(pl.multiple_of(z * rows, rows), rows)] = new[i]
            else:
                slot = pl.multiple_of((z + 1 + cz) * rows, rows)
                pre[PLACE[i], pl.ds(slot, rows)] = new[i]
            if cy:
                a = SIGNS.index(cy)
                place = z if cz == 0 else lax.rem(z + cz + depth, depth)
                edge = width - 1 if cy == 1 else 0
                pack(a, new[i], edge, Y_GROUP[a].index(i) * depth + place)
        return tuple(packed)

    halo = []

    def send(src, dst, offset):
        copy = pltpu.make_async_remote_copy(
            src_ref=src,
            dst_ref=dst,
            send_sem=send_sem.at[len(halo)],
            recv_sem=recv_sem.at[len(halo)],
            device_id=at(offset),
            device_id_type=MESH,
        )
        copy.start()
        halo.append(copy)

    def shift(i, value):
        cx, cy, _ = VELOCITY[i]
        if cx:
            value = pltpu.roll(value, cx % rows, 0)
        if cy:
            value = pltpu.roll(value, cy % width, 1)
        return value

    zero = jnp.zeros((rows, width), F32)
    packed = lax.fori_loop(0, depth, collide, (zero, zero), unroll=UNROLL)
    for a, s in enumerate(SIGNS):
        edge = rows - 1 if a == 0 else 0
        for k, i in enumerate(X_GROUP[a]):
            _, cy, cz = VELOCITY[i]
            line = post[PLACE[i], pl.ds(edge, depth, stride=rows), :]
            if cy:
                line = pltpu.roll(line, cy % width, 1)
            xs[a, k] = line
            if cz:
                place = depth - 1 if cz == 1 else 0
                xe[a, SIGNS.index(cz)] = line[place : place + 1]
        send(xs.at[a], xh.at[a], (s, 0, 0))
    for a, s in enumerate(SIGNS):
        z, source, target = (depth - 1, depth + 1, 1) if a == 0 else (0, 0, depth)
        for i in Z_GROUP[a]:
            if VELOCITY[i][0] or VELOCITY[i][1]:
                value = shift(i, post[PLACE[i], z * rows : (z + 1) * rows, :])
                pre[PLACE[i], source * rows : (source + 1) * rows, :] = value
        tile = packed[a]
        for j, i in enumerate(Y_GROUP[a]):
            cx = VELOCITY[i][0]
            if cx:
                own = (lane >= j * depth) & (lane < (j + 1) * depth)
                tile = jnp.where(own, pltpu.roll(packed[a], cx % rows, 0), tile)
        ys[a] = tile
        for b in range(2):
            wrap = 0 if b == 0 else rows - 1
            yr[a, b] = tile[wrap : wrap + 1]

    for a, s in enumerate(SIGNS):
        send(ys.at[a], yh.at[a], (0, s, 0))
        for b, t in enumerate(SIGNS):
            send(yr.at[a, b], yrh.at[a, b], (t, s, 0))
            send(ys.at[a], yzh.at[a, b], (0, s, t))
            send(xe.at[a, b], xeh.at[a, b], (s, 0, t))
        group = pl.ds(a * 5, 5)
        source, target = (depth + 1, 1) if a == 0 else (0, depth)
        send(
            pre.at[group, pl.ds(source * rows, rows)],
            pre.at[group, pl.ds(target * rows, rows)],
            (0, 0, s),
        )


    masked = []
    for a in range(2):
        on_x = cell_x == (rows - 1 if a == 0 else 0)
        for b in range(2):
            on_level = cell_z == (depth - 1 if b == 0 else 0)
            masked.append(jnp.where(on_x & on_level, table, 0.0))
    high, low = halves(jnp.concatenate(masked, axis=0))
    edge_rows = dot_nt(high, pick_col) + dot_nt(low, pick_col)
    for a, s in enumerate(SIGNS):
        for b, t in enumerate(SIGNS):
            first = (2 * a + b) * MODE_ROWS
            edges[a, b] = edge_rows[first : first + MODE_ROWS]
            pass_on(edges.at[a, b], edges_in.at[a, b], (s, 0, t))


    row_id = lax.broadcasted_iota(jnp.int32, (rows, n_surf), 0)
    sides = jnp.concatenate(
        [
            jnp.where((row_id == cell_x) & (col == (width - 1 if a == 0 else 0)), 1.0, 0.0)
            for a in range(2)
        ],
        axis=0,
    ).astype(BF16)
    on_z = lax.rem(spot, depth) == cell_z
    for t in range(2):
        spread_rows = jnp.concatenate(
            [
                jnp.broadcast_to(
                    table[t * groups + g : t * groups + g + 1, :]
                    if t * groups + g < MODES
                    else jnp.zeros((1, n_surf), F32),
                    (depth, n_surf),
                )
                for g in range(groups)
            ],
            axis=0,
        )
        high, low = halves(jnp.where(on_z, spread_rows, 0.0))
        shared = dot_nt(sides, high) + dot_nt(sides, low)
        for a in range(2):
            faces[a, t] = shared[a * rows : (a + 1) * rows]
            for b in range(2):
                edge = a * rows + (rows - 1 if b == 0 else 0)
                corners[a, b, t] = shared[edge : edge + 1]

    for a, s in enumerate(SIGNS):
        pass_on(faces.at[a], flux_y.at[a], (0, s, 0))
        for b, t in enumerate(SIGNS):
            pass_on(corners.at[a, b], corners_in.at[a, b], (t, s, 0))


    half = cells // 2
    in_row = lax.broadcasted_iota(jnp.int32, (half, n_surf), 0) == lax.rem(row, half)
    in_row = jnp.where(in_row, 1.0, 0.0).astype(BF16).reshape(half // 16, 16, n_surf)
    wide = lax.broadcasted_iota(jnp.int32, (2 * width, n_surf), 0)
    pick_half = jnp.where(wide == lax.div(row, half) * width + col, 1.0, 0.0).astype(BF16)

    def scatter(step, carry):
        parts = []
        for k in range(PER_DOT):
            line = jnp.broadcast_to(mine[step * PER_DOT + k], (16, n_surf))
            for value in halves(line):
                parts.append((in_row * value[None]).reshape(half, n_surf))
        found = dot_nt(jnp.concatenate(parts, axis=0), pick_half)
        for k in range(PER_DOT):
            first = 2 * k * half
            flux = found[first : first + half] + found[first + half : first + 2 * half]
            for h in range(2):
                value = flux[:, h * width : (h + 1) * width].reshape(depth // 2, rows, width)
                flux_m[step * PER_DOT + k, pl.ds(1 + h * (depth // 2), depth // 2)] = value
        return carry

    lax.fori_loop(0, MODES // PER_DOT, scatter, 0, unroll=True)
    for a, s in enumerate(SIGNS):
        source, target = (depth, 0) if a == 0 else (1, depth + 1)
        pass_on(flux_m.at[:, source], flux_m.at[:, target], (0, 0, s))

    for z in range(depth):
        for i in range(19):
            cx, cy, cz = VELOCITY[i]
            if (cx or cy) and 0 <= z + cz < depth:
                slot = (z + 1 + cz) * rows
                value = shift(i, post[PLACE[i], z * rows : (z + 1) * rows, :])
                pre[PLACE[i], slot : slot + rows, :] = value

    for copy in loads[len(small) + N_LOADS + 1 :]:
        copy.wait()
    mode_id = lax.broadcasted_iota(jnp.int32, (MODE_ROWS, PANELS), 0)
    diagonal = lax.broadcasted_iota(jnp.int32, (MODE_ROWS, MODES), 0) == lax.broadcasted_iota(
        jnp.int32, (MODE_ROWS, MODES), 1
    )
    factor = jnp.sum(jnp.where(diagonal, compliance[...], 0.0), axis=1, keepdims=True)
    drive_out[...] = jnp.where(panel_mode[...] == mode_id, factor, 0.0)

    for n in range(1, len(stages)):
        stage_start(n, stage_sum(n - 1))

    for copy in surfels[:2]:
        copy.wait()
    level_id = lax.broadcasted_iota(jnp.int32, (depth, n_surf), 0)
    for a in range(2):
        other = theirs[a, CELL_ROW].astype(jnp.int32)
        pick = jnp.where(spot == lax.rem(other, width), 1.0, 0.0).astype(BF16)
        on_x = lax.rem(lax.div(other, width), rows) == (rows - 1 if a == 0 else 0)
        on_face = (level_id == lax.div(other, width * rows)) & on_x
        lines = jnp.concatenate(
            [jnp.where(on_face, theirs[a, m], 0.0) for m in range(MODES)], axis=0
        )
        high, low = halves(lines)
        lines = dot_nt(high, pick) + dot_nt(low, pick)
        for m in range(MODES):
            flux_x[a, m, 0:depth, :] = lines[m * depth : (m + 1) * depth]
            flux_x[a, m, HIGH + 1 :, :] = jnp.zeros((rows - 2, width), F32)
    flux_c[:, 4:, :] = jnp.zeros((2, rows - 4, width), F32)

    for copy in halo:
        copy.wait()

    columns = []
    for a in range(2):
        result = yh[a]
        for j, i in enumerate(Y_GROUP[a]):
            cx, _, cz = VELOCITY[i]
            if cx:
                own = (lane >= j * depth) & (lane < (j + 1) * depth)
                own = own & (sub == (0 if cx == 1 else rows - 1))
                result = jnp.where(own, yrh[a, SIGNS.index(cx)], result)
            if cz:
                place = j * depth if cz == 1 else (j + 1) * depth - 1
                result = jnp.where(lane == place, yzh[a, SIGNS.index(cz)], result)
        columns.append(result)
        column_out[a] = result
    for a in range(2):
        wrap = 0 if a == 0 else rows - 1
        for k, i in enumerate(X_GROUP[a]):
            cz = VELOCITY[i][2]
            first = (1 + cz) * rows + wrap
            pre[PLACE[i], pl.ds(first, depth, stride=rows), :] = xh[a, k]
            if cz:
                first = (1 if cz == 1 else depth) * rows + wrap
                pre[PLACE[i], first : first + 1, :] = xeh[a, SIGNS.index(cz)]
    for a in range(2):
        for j, i in enumerate(Y_GROUP[a]):
            if VELOCITY[i][0]:
                continue
            at_edge = lane == (0 if a == 0 else width - 1)
            for z in range(depth):
                tile_rows = pl.ds((z + 1) * rows, rows)
                place = j * depth + z
                column = jnp.broadcast_to(columns[a][:, place : place + 1], (rows, width))
                pre[PLACE[i], tile_rows] = jnp.where(at_edge, column, pre[PLACE[i], tile_rows])


    for copy in surfels[2:]:
        copy.wait()
    for a in range(2):
        for b in range(2):
            place = LOW if b == 0 else HIGH
            for m in range(MODES):
                flux_x[a, m, place : place + 1, :] = edges_in[a, b, m : m + 1, :]
            for t in range(2):
                k = 2 * a + b
                flux_c[t, k : k + 1, :] = corners_in[a, b, t]

    total_out[...] = stage_sum(len(stages) - 1)


MOVED = X_GROUP[0] + X_GROUP[1]
FIXED_RUNS = ((0, 1), (3, 2), (5, 1), (6, 1), (15, 1), (16, 1), (17, 1), (18, 1))
MOVED_RUNS = ((1, 2), (7, 8))
N_CUTS = 4


def apply(pre, flux_m, flux_x, flux_y, flux_c, column, total, drive, out, force_out, amp_out, stage, force, amplitude, sem):
    depth, rows, width = flux_m.shape[1] - 2, flux_m.shape[2], flux_m.shape[3]
    copies = []

    def write(src, dst):
        copy = pltpu.make_async_copy(src, dst, sem.at[len(copies)])
        copy.start()
        copies.append(copy)

    for first, count in FIXED_RUNS:
        run = pl.ds(PLACE[first], count)
        write(pre.at[run, pl.ds(rows, depth * rows)], out.at[pl.ds(first, count)])

    lane = lax.broadcasted_iota(jnp.int32, (rows, width), 1)
    sub = lax.broadcasted_iota(jnp.int32, (rows, width), 0)
    load = total[:, :PANELS]
    force[...] = load
    write(force, force_out)
    amp = jnp.sum(drive[...] * load, axis=1, keepdims=True)
    diagonal = lax.broadcasted_iota(jnp.int32, (MODE_ROWS, MODES), 0) == lax.broadcasted_iota(
        jnp.int32, (MODE_ROWS, MODES), 1
    )
    amps = [jnp.broadcast_to(amp[m : m + 1], (rows, width)) for m in range(MODES)]
    groups = width // depth
    gains = []
    for t in range(2):
        gain = jnp.zeros((rows, width), F32)
        for m in range(t * groups, min(MODES, (t + 1) * groups)):
            gain = jnp.where(lane // depth == m - t * groups, amps[m], gain)
        gains.append(gain)

    def gather(first, second):
        tile = first * gains[0] + second * gains[1]
        step = depth
        while step < width:
            tile = tile + pltpu.roll(tile, step, 1)
            step *= 2
        return tile

    corner = gather(flux_c[0], flux_c[1])
    columns = {}
    for a, s in enumerate(SIGNS):
        face = gather(flux_y[a, 0], flux_y[a, 1])
        for b, t in enumerate(SIGNS):
            edge = corner[2 * a + b : 2 * a + b + 1]
            moved = pltpu.roll(face, t % rows, 0)
            moved = jnp.where(sub == (0 if t == 1 else rows - 1), edge, moved)
            i = VELOCITY.index((t, s, 0))
            columns[t, s] = column[a] + COEF[i] * moved

    def weigh(terms):
        return tree_sum([amps[m] * terms[m] for m in range(MODES)])

    lines = [
        [
            weigh([flux_x[a, m, r * rows : (r + 1) * rows, :] for m in range(MODES)])
            for r in range(3)
        ]
        for a in range(2)
    ]

    part = depth // N_CUTS
    for slot in range(depth + 2):
        flux = weigh([flux_m[m, slot] for m in range(MODES)])
        place = LOW if slot == 0 else HIGH if slot == depth + 1 else slot - 1
        for a, s in enumerate(SIGNS):
            line = lines[a][place // rows][place % rows : place % rows + 1]
            moved = pltpu.roll(flux, s % rows, 0)
            moved = jnp.where(sub == (0 if s == 1 else rows - 1), line, moved)
            for i in X_GROUP[a]:
                _, cy, cz = VELOCITY[i]
                z = slot - 1 + cz
                if not 0 <= z < depth:
                    continue
                value = pltpu.roll(moved, cy % width, 1) if cy else moved
                value = pre[PLACE[i], (z + 1) * rows : (z + 2) * rows, :] + COEF[i] * value
                if cy:
                    first = Y_GROUP[SIGNS.index(cy)].index(i) * depth + z
                    beside = columns[s, cy][:, first : first + 1]
                    beside = jnp.broadcast_to(beside, (rows, width))
                    value = jnp.where(lane == (0 if cy == 1 else width - 1), beside, value)
                stage[i, z * rows : (z + 1) * rows] = value
        if slot >= 2 and (slot - 1) % part == 0:
            cut = pl.ds((slot - 1 - part) * rows, part * rows)
            for first, count in MOVED_RUNS:
                run = pl.ds(first, count)
                write(stage.at[run, cut], out.at[run, cut])
    amplitude[...] = jnp.sum(jnp.where(diagonal, amp, 0.0), axis=0, keepdims=True)
    write(amplitude, amp_out)
    for copy in copies:
        copy.wait()


def per_device(sizes, pops, solid, cell, panel, area, shapes, panel_mode, compliance):
    depth, rows, width = pops.shape[1:]
    n_surf = cell.shape[-1]
    stages = stages_of(sizes)
    n_slots = max(len(stage_offsets(stage, sizes)) + 1 for stage in stages)
    vmem = pl.BlockSpec(memory_space=pltpu.VMEM)
    hbm = pl.BlockSpec(memory_space=pltpu.HBM)
    tile = (rows, width)
    dma = pltpu.SemaphoreType.DMA
    passed = pl.pallas_call(
        functools.partial(exchange, sizes),
        out_shape=(
            jax.ShapeDtypeStruct((19, (depth + 2) * rows, width), F32),
            jax.ShapeDtypeStruct((MODES, depth + 2) + tile, F32),
            jax.ShapeDtypeStruct((2, MODES, depth + rows, width), F32),
            jax.ShapeDtypeStruct((2, 2) + tile, F32),
            jax.ShapeDtypeStruct((2,) + tile, F32),
            jax.ShapeDtypeStruct((2,) + tile, F32),
            jax.ShapeDtypeStruct((1, width), F32),
            jax.ShapeDtypeStruct((MODE_ROWS, PANELS), F32),
        ),
        in_specs=[hbm] * 8,
        out_specs=(vmem,) * 8,
        scratch_shapes=[
            pltpu.VMEM(pops.shape, F32),
            pltpu.VMEM(solid.shape, jnp.int32),
            pltpu.VMEM((1, n_surf), jnp.int32),
            pltpu.VMEM((1, n_surf), jnp.int32),
            pltpu.VMEM((1, n_surf), F32),
            pltpu.VMEM((MODES, 1, n_surf), F32),
            pltpu.VMEM((1, PANELS), jnp.int32),
            pltpu.VMEM((1, MODES), F32),
            pltpu.VMEM((MODES + 1, 1, n_surf), F32),
            dma((7 + N_LOADS,)),
            pltpu.VMEM((19, depth * rows, width), F32),
            pltpu.VMEM((depth * rows, width), F32),
            pltpu.VMEM((2, 5, depth, width), F32),
            pltpu.VMEM((2, 5, depth, width), F32),
            pltpu.VMEM((2, 2, 1, width), F32),
            pltpu.VMEM((2, 2, 1, width), F32),
            pltpu.VMEM((2,) + tile, F32),
            pltpu.VMEM((2,) + tile, F32),
            pltpu.VMEM((2, 2, 1, width), F32),
            pltpu.VMEM((2, 2, 1, width), F32),
            pltpu.VMEM((2, 2) + tile, F32),
            pltpu.VMEM((2, MODES + 1, 1, n_surf), F32),
            pltpu.VMEM((2, 2, MODE_ROWS, width), F32),
            pltpu.VMEM((2, 2, MODE_ROWS, width), F32),
            pltpu.VMEM((2, 2) + tile, F32),
            pltpu.VMEM((2, 2, 2, 1, width), F32),
            pltpu.VMEM((2, 2, 2, 1, width), F32),
            dma((N_SURF,)),
            dma((N_SURF,)),
            pltpu.VMEM((len(stages), n_slots, 1, width), F32),
            dma((N_HALO,)),
            dma((N_HALO,)),
            dma((len(stages),)),
            dma((len(stages),)),
        ],
        compiler_params=pltpu.CompilerParams(
            collective_id=0, has_side_effects=True, vmem_limit_bytes=24 * 1024 * 1024
        ),
    )(
        *(
            pltpu.with_memory_space_constraint(x, pltpu.HBM)
            for x in (
                pops,
                solid,
                cell.reshape(1, n_surf),
                panel.reshape(1, n_surf),
                area.reshape(1, n_surf),
                shapes.reshape(MODES, 1, n_surf),
                panel_mode.reshape(1, PANELS),
                compliance.reshape(1, MODES),
            )
        )
    )
    read, force, amp = pl.pallas_call(
        apply,
        out_shape=(
            jax.ShapeDtypeStruct((19, depth * rows, width), F32),
            jax.ShapeDtypeStruct((1, PANELS), F32),
            jax.ShapeDtypeStruct((1, MODES), F32),
        ),
        in_specs=[vmem] * 8,
        out_specs=(hbm,) * 3,
        scratch_shapes=[
            pltpu.VMEM((19, depth * rows, width), F32),
            pltpu.VMEM((1, PANELS), F32),
            pltpu.VMEM((1, MODES), F32),
            dma((len(FIXED_RUNS) + len(MOVED_RUNS) * N_CUTS + 2,)),
        ],
        compiler_params=pltpu.CompilerParams(vmem_limit_bytes=8 * 1024 * 1024),
    )(*passed)
    return read.reshape(pops.shape), force.reshape(PANELS), amp.reshape(MODES)


def solution(mesh):
    placed = (
        P(None, "gz", "gx", "gy"),
        P("gz", "gx", "gy"),
        P("gz", "gx", "gy", None),
        P("gz", "gx", "gy", None),
        P("gz", "gx", "gy", None),
        P("gz", "gx", "gy", None, None),
        P(),
        P(),
    )
    return jax.shard_map(
        functools.partial(per_device, tuple(mesh.shape[a] for a in AXES)),
        mesh=mesh,
        in_specs=placed,
        out_specs=(P(None, "gz", "gx", "gy"), P(), P()),
        check_vma=False,
    )
```

```python
import functools

import jax
import jax.numpy as jnp
from jax import lax
from jax.experimental import pallas as pl
from jax.experimental.pallas import tpu as pltpu
from jax.sharding import PartitionSpec as P

PANELS = 40
MODES = 12
VELOCITY = (
    (0, 0, 0),
    (1, 0, 0),
    (-1, 0, 0),
    (0, 1, 0),
    (0, -1, 0),
    (0, 0, 1),
    (0, 0, -1),
    (1, 1, 0),
    (-1, -1, 0),
    (1, -1, 0),
    (-1, 1, 0),
    (1, 0, 1),
    (-1, 0, -1),
    (1, 0, -1),
    (-1, 0, 1),
    (0, 1, 1),
    (0, -1, -1),
    (0, 1, -1),
    (0, -1, 1),
)
WEIGHTS = (1.0 / 3.0,) + (1.0 / 18.0,) * 6 + (1.0 / 36.0,) * 12
OMEGA = 1.0 / 0.6
WALL_SCALE = 0.02
COEF = tuple(6.0 * w * v[0] for w, v in zip(WEIGHTS, VELOCITY))
SIGNS = (1, -1)


def moving(axis, sign):
    return tuple(i for i in range(19) if VELOCITY[i][axis] == sign)


X_GROUP = tuple(moving(0, s) for s in SIGNS)
Y_GROUP = tuple(moving(1, s) for s in SIGNS)
Z_GROUP = tuple(moving(2, s) for s in SIGNS)
ORDER = Z_GROUP[0] + Z_GROUP[1] + tuple(i for i in range(19) if VELOCITY[i][2] == 0)
PLACE = tuple(ORDER.index(i) for i in range(19))
AXES = ("gx", "gy", "gz")
MESH = pl.DeviceIdType.MESH
N_LOADS = 2
MODE_ROWS = 16
CELL_ROW = MODES
LOW, HIGH = 16, 17
F32 = jnp.float32
BF16 = jnp.bfloat16


def stages_of(sizes):
    if sizes[0] * sizes[1] * sizes[2] <= 64:
        return (AXES,)
    return (("gx",), ("gy", "gz"))


def halves(x):
    high = x.astype(BF16)
    return high, (x - high.astype(F32)).astype(BF16)


def dot(a, b):
    return jnp.dot(a, b, preferred_element_type=F32)


def dot_nt(a, b):
    return lax.dot_general(a, b, (((1,), (1,)), ((), ())), preferred_element_type=F32)


def stage_offsets(stage, sizes):
    result = [(0, 0, 0)]
    for dim, axis in enumerate(AXES):
        if axis in stage:
            result = [
                tuple(k if d == dim else o[d] for d in range(3))
                for o in result
                for k in range(sizes[dim])
            ]
    return [o for o in result if o != (0, 0, 0)]


def offsets_of(sizes):
    found = []
    for i in range(1, 19):
        found.append(tuple(c % n for c, n in zip(VELOCITY[i], sizes)))
    for stage in stages_of(sizes):
        found += stage_offsets(stage, sizes)
    return sorted(set(found))


def tree_sum(terms):
    while len(terms) > 1:
        terms = [sum(terms[k + 1 : k + 2], terms[k]) for k in range(0, len(terms), 2)]
    return terms[0]


UNROLL = 4
N_HALO = 18
PER_DOT = 2
N_SURF = 2 + 4 + 2 + 4 + 2


def exchange(
    sizes,
    pops_in,
    solid_in,
    cell_in,
    panel_in,
    area_in,
    shapes_in,
    panel_mode_in,
    compliance_in,
    pre,
    flux_m,
    flux_x,
    flux_y,
    flux_c,
    column_out,
    total_out,
    drive_out,
    pops,
    solid,
    cell,
    panel,
    area,
    shape_rows,
    panel_mode,
    compliance,
    mine,
    load_sem,
    post,
    dens,
    xs,
    xh,
    xe,
    xeh,
    ys,
    yh,
    yr,
    yrh,
    yzh,
    theirs,
    edges,
    edges_in,
    faces,
    corners,
    corners_in,
    surf_send,
    surf_recv,
    slots,
    send_sem,
    recv_sem,
    stage_send,
    stage_recv,
):
    depth, rows, width = pops.shape[1:]
    cells = depth * rows
    groups = width // depth
    here = tuple(lax.axis_index(a) for a in AXES)
    stages = stages_of(sizes)
    targets = {}

    def at(offset):
        key = tuple(o % n for o, n in zip(offset, sizes))
        if key not in targets:
            targets[key] = tuple(
                lax.rem(h + o, n) if o else h for h, o, n in zip(here, key, sizes)
            )
        return targets[key]

    partners = offsets_of(sizes)
    barrier = pltpu.get_barrier_semaphore()
    for offset in partners:
        pl.semaphore_signal(barrier, inc=1, device_id=at(offset), device_id_type=MESH)

    small = [(cell_in, cell), (panel_in, panel), (area_in, area), (shapes_in, shape_rows)]
    starts = [19 * n // N_LOADS for n in range(N_LOADS + 1)]
    cuts = [pl.ds(a, b - a) for a, b in zip(starts[:-1], starts[1:])]
    big = [(pops_in.at[c], pops.at[c]) for c in cuts]
    late = [(solid_in, solid), (panel_mode_in, panel_mode), (compliance_in, compliance)]
    loads = []
    for n, (src, dst) in enumerate(small + big + late):
        loads.append(pltpu.make_async_copy(src, dst, load_sem.at[n]))
        loads[n].start()

    lane = lax.broadcasted_iota(jnp.int32, (rows, width), 1)
    sub = lax.broadcasted_iota(jnp.int32, (rows, width), 0)

    for copy in loads[: len(small)]:
        copy.wait()
    n_surf = cell.shape[1]
    live = panel[...] >= 0
    col = lax.rem(cell[...], width)
    row = lax.div(cell[...], width)
    cell_x = lax.rem(row, rows)
    cell_z = lax.div(row, rows)
    spot = lax.broadcasted_iota(jnp.int32, (width, n_surf), 0)
    pick_col = jnp.where(spot == col, 1.0, 0.0).astype(BF16)
    on_row = lax.broadcasted_iota(jnp.int32, (cells, n_surf), 0) == row

    for n in range(N_LOADS):
        loads[len(small) + n].wait()
        for z in range(depth):
            place = slice(z * rows, (z + 1) * rows)
            density = tree_sum([pops[i, z] for i in range(starts[n], starts[n + 1])])
            dens[place, :] = density if n == 0 else dens[place, :] + density
    def stage_start(n, value):
        stage = stages[n]
        index = 0
        for dim, axis in enumerate(AXES):
            if axis in stage:
                index = index * sizes[dim] + here[dim]
        slots[n, index] = value
        for offset in stage_offsets(stage, sizes):
            pltpu.make_async_remote_copy(
                src_ref=slots.at[n, index],
                dst_ref=slots.at[n, index],
                send_sem=stage_send.at[n],
                recv_sem=stage_recv.at[n],
                device_id=at(offset),
                device_id_type=MESH,
            ).start()

    def stage_sum(n):
        count = len(stage_offsets(stages[n], sizes))
        whole = pltpu.make_async_remote_copy(
            src_ref=slots.at[n, pl.ds(0, count)],
            dst_ref=slots.at[n, pl.ds(0, count)],
            send_sem=stage_send.at[n],
            recv_sem=stage_recv.at[n],
            device_id=at(stage_offsets(stages[n], sizes)[0]),
            device_id_type=MESH,
        )
        whole.wait_recv()
        whole.wait_send()
        return tree_sum([slots[n, k] for k in range(count + 1)])

    surfels = []

    def pass_on(src, dst, offset):
        copy = pltpu.make_async_remote_copy(
            src_ref=src,
            dst_ref=dst,
            send_sem=surf_send.at[len(surfels)],
            recv_sem=surf_recv.at[len(surfels)],
            device_id=at(offset),
            device_id_type=MESH,
        )
        copy.start()
        surfels.append(copy)

    gauge_high, gauge_low = halves(dens[...] - 1.0)
    by_row = dot(gauge_high, pick_col) + dot(gauge_low, pick_col)
    excess = jnp.sum(jnp.where(on_row, by_row, 0.0), axis=0, keepdims=True)
    contrib = jnp.where(live, area[...] * (excess / 3.0), 0.0)
    pick_panel = jnp.where(spot == panel[...], 1.0, 0.0).astype(BF16)
    contrib_high, contrib_low = halves(jnp.broadcast_to(contrib, (8, n_surf)))
    partial = dot_nt(contrib_high, pick_panel) + dot_nt(contrib_low, pick_panel)
    partial = partial[0:1]


    scale = WALL_SCALE * (excess + 1.0)
    table = [jnp.where(live, shape_rows[m] * scale, 0.0) for m in range(MODES)]
    table.append(cell[...].astype(F32))
    for m, line in enumerate(table):
        mine[m] = line
    table = jnp.concatenate(
        table[:MODES] + [jnp.zeros((MODE_ROWS - MODES, n_surf), F32)], axis=0
    )

    pl.semaphore_wait(barrier, len(partners))


    for a, s in enumerate(SIGNS):
        pass_on(mine, theirs.at[a], (s, 0, 0))


    stage_start(0, partial)


    loads[len(small) + N_LOADS].wait()

    def collide(z, packed):
        f = [pops[i, z] for i in range(19)]
        density = dens[pl.ds(pl.multiple_of(z * rows, rows), rows)]
        inverse = 1.0 / density
        u = []
        for axis in range(3):
            plus, minus = moving(axis, 1), moving(axis, -1)
            total = f[plus[0]] - f[minus[0]]
            for i, j in zip(plus[1:], minus[1:]):
                total = total + (f[i] - f[j])
            u.append(total * inverse)
        base = 1.0 - 1.5 * (u[0] * u[0] + u[1] * u[1] + u[2] * u[2])
        fixed = solid[z] == 1
        scaled = [OMEGA * w * density for w in WEIGHTS]
        new = [None] * 19
        new[0] = jnp.where(fixed, f[0], (1.0 - OMEGA) * f[0] + scaled[0] * base)
        for i in range(1, 19, 2):
            proj = None
            for axis in range(3):
                comp = VELOCITY[i][axis]
                if comp:
                    term = u[axis] if comp == 1 else -u[axis]
                    proj = term if proj is None else proj + term
            even = scaled[i] * (base + 4.5 * (proj * proj))
            odd = scaled[i] * (3.0 * proj)
            new[i] = jnp.where(fixed, f[i + 1], (1.0 - OMEGA) * f[i] + (even + odd))
            new[i + 1] = jnp.where(fixed, f[i], (1.0 - OMEGA) * f[i + 1] + (even - odd))
        packed = list(packed)

        def pack(a, value, edge, place):
            column = jnp.broadcast_to(value[:, edge : edge + 1], (rows, width))
            packed[a] = jnp.where(lane == place, column, packed[a])

        for i in range(19):
            cx, cy, cz = VELOCITY[i]
            if cx or cy:
                post[PLACE[i], pl.ds(pl.multiple_of(z * rows, rows), rows)] = new[i]
            else:
                slot = pl.multiple_of((z + 1 + cz) * rows, rows)
                pre[PLACE[i], pl.ds(slot, rows)] = new[i]
            if cy:
                a = SIGNS.index(cy)
                place = z if cz == 0 else lax.rem(z + cz + depth, depth)
                edge = width - 1 if cy == 1 else 0
                pack(a, new[i], edge, Y_GROUP[a].index(i) * depth + place)
        return tuple(packed)

    halo = []

    def send(src, dst, offset):
        copy = pltpu.make_async_remote_copy(
            src_ref=src,
            dst_ref=dst,
            send_sem=send_sem.at[len(halo)],
            recv_sem=recv_sem.at[len(halo)],
            device_id=at(offset),
            device_id_type=MESH,
        )
        copy.start()
        halo.append(copy)

    def shift(i, value):
        cx, cy, _ = VELOCITY[i]
        if cx:
            value = pltpu.roll(value, cx % rows, 0)
        if cy:
            value = pltpu.roll(value, cy % width, 1)
        return value

    zero = jnp.zeros((rows, width), F32)
    packed = lax.fori_loop(0, depth, collide, (zero, zero), unroll=UNROLL)
    for a, s in enumerate(SIGNS):
        edge = rows - 1 if a == 0 else 0
        for k, i in enumerate(X_GROUP[a]):
            _, cy, cz = VELOCITY[i]
            line = post[PLACE[i], pl.ds(edge, depth, stride=rows), :]
            if cy:
                line = pltpu.roll(line, cy % width, 1)
            xs[a, k] = line
            if cz:
                place = depth - 1 if cz == 1 else 0
                xe[a, SIGNS.index(cz)] = line[place : place + 1]
        send(xs.at[a], xh.at[a], (s, 0, 0))
    for a, s in enumerate(SIGNS):
        z, source, target = (depth - 1, depth + 1, 1) if a == 0 else (0, 0, depth)
        for i in Z_GROUP[a]:
            if VELOCITY[i][0] or VELOCITY[i][1]:
                value = shift(i, post[PLACE[i], z * rows : (z + 1) * rows, :])
                pre[PLACE[i], source * rows : (source + 1) * rows, :] = value
        tile = packed[a]
        for j, i in enumerate(Y_GROUP[a]):
            cx = VELOCITY[i][0]
            if cx:
                own = (lane >= j * depth) & (lane < (j + 1) * depth)
                tile = jnp.where(own, pltpu.roll(packed[a], cx % rows, 0), tile)
        ys[a] = tile
        for b in range(2):
            wrap = 0 if b == 0 else rows - 1
            yr[a, b] = tile[wrap : wrap + 1]

    for a, s in enumerate(SIGNS):
        send(ys.at[a], yh.at[a], (0, s, 0))
        for b, t in enumerate(SIGNS):
            send(yr.at[a, b], yrh.at[a, b], (t, s, 0))
            send(ys.at[a], yzh.at[a, b], (0, s, t))
            send(xe.at[a, b], xeh.at[a, b], (s, 0, t))
        group = pl.ds(a * 5, 5)
        source, target = (depth + 1, 1) if a == 0 else (0, depth)
        send(
            pre.at[group, pl.ds(source * rows, rows)],
            pre.at[group, pl.ds(target * rows, rows)],
            (0, 0, s),
        )


    masked = []
    for a in range(2):
        on_x = cell_x == (rows - 1 if a == 0 else 0)
        for b in range(2):
            on_level = cell_z == (depth - 1 if b == 0 else 0)
            masked.append(jnp.where(on_x & on_level, table, 0.0))
    high, low = halves(jnp.concatenate(masked, axis=0))
    edge_rows = dot_nt(high, pick_col) + dot_nt(low, pick_col)
    for a, s in enumerate(SIGNS):
        for b, t in enumerate(SIGNS):
            first = (2 * a + b) * MODE_ROWS
            for m in range(MODES):
                edges[a, b, m] = edge_rows[first + m : first + m + 1]
            pass_on(edges.at[a, b], edges_in.at[a, b], (s, 0, t))


    row_id = lax.broadcasted_iota(jnp.int32, (rows, n_surf), 0)
    sides = jnp.concatenate(
        [
            jnp.where((row_id == cell_x) & (col == (width - 1 if a == 0 else 0)), 1.0, 0.0)
            for a in range(2)
        ],
        axis=0,
    ).astype(BF16)
    on_z = lax.rem(spot, depth) == cell_z
    for t in range(2):
        spread_rows = jnp.concatenate(
            [
                jnp.broadcast_to(
                    table[t * groups + g : t * groups + g + 1, :]
                    if t * groups + g < MODES
                    else jnp.zeros((1, n_surf), F32),
                    (depth, n_surf),
                )
                for g in range(groups)
            ],
            axis=0,
        )
        high, low = halves(jnp.where(on_z, spread_rows, 0.0))
        shared = dot_nt(sides, high) + dot_nt(sides, low)
        for a in range(2):
            faces[a, t] = shared[a * rows : (a + 1) * rows]
            for b in range(2):
                edge = a * rows + (rows - 1 if b == 0 else 0)
                corners[a, b, t] = shared[edge : edge + 1]

    for a, s in enumerate(SIGNS):
        pass_on(faces.at[a], flux_y.at[a], (0, s, 0))
        for b, t in enumerate(SIGNS):
            pass_on(corners.at[a, b], corners_in.at[a, b], (t, s, 0))


    half = cells // 2
    in_row = lax.broadcasted_iota(jnp.int32, (half, n_surf), 0) == lax.rem(row, half)
    in_row = jnp.where(in_row, 1.0, 0.0).astype(BF16).reshape(half // 16, 16, n_surf)
    wide = lax.broadcasted_iota(jnp.int32, (2 * width, n_surf), 0)
    pick_half = jnp.where(wide == lax.div(row, half) * width + col, 1.0, 0.0).astype(BF16)

    def scatter(step, carry):
        parts = []
        for k in range(PER_DOT):
            line = jnp.broadcast_to(mine[step * PER_DOT + k], (16, n_surf))
            for value in halves(line):
                parts.append((in_row * value[None]).reshape(half, n_surf))
        found = dot_nt(jnp.concatenate(parts, axis=0), pick_half)
        for k in range(PER_DOT):
            first = 2 * k * half
            flux = found[first : first + half] + found[first + half : first + 2 * half]
            for h in range(2):
                value = flux[:, h * width : (h + 1) * width].reshape(depth // 2, rows, width)
                flux_m[step * PER_DOT + k, pl.ds(1 + h * (depth // 2), depth // 2)] = value
        return carry

    lax.fori_loop(0, MODES // PER_DOT, scatter, 0, unroll=True)
    for a, s in enumerate(SIGNS):
        source, target = (depth, 0) if a == 0 else (1, depth + 1)
        pass_on(flux_m.at[:, source], flux_m.at[:, target], (0, 0, s))

    for z in range(depth):
        for i in range(19):
            cx, cy, cz = VELOCITY[i]
            if (cx or cy) and 0 <= z + cz < depth:
                slot = (z + 1 + cz) * rows
                value = shift(i, post[PLACE[i], z * rows : (z + 1) * rows, :])
                pre[PLACE[i], slot : slot + rows, :] = value

    for copy in loads[len(small) + N_LOADS + 1 :]:
        copy.wait()
    mode_id = lax.broadcasted_iota(jnp.int32, (MODE_ROWS, PANELS), 0)
    diagonal = lax.broadcasted_iota(jnp.int32, (MODE_ROWS, MODES), 0) == lax.broadcasted_iota(
        jnp.int32, (MODE_ROWS, MODES), 1
    )
    factor = jnp.sum(jnp.where(diagonal, compliance[...], 0.0), axis=1, keepdims=True)
    drive_out[...] = jnp.where(panel_mode[...] == mode_id, factor, 0.0)

    for n in range(1, len(stages)):
        stage_start(n, stage_sum(n - 1))

    for copy in surfels[:2]:
        copy.wait()
    level_id = lax.broadcasted_iota(jnp.int32, (depth, n_surf), 0)
    for a in range(2):
        other = theirs[a, CELL_ROW].astype(jnp.int32)
        pick = jnp.where(spot == lax.rem(other, width), 1.0, 0.0).astype(BF16)
        on_x = lax.rem(lax.div(other, width), rows) == (rows - 1 if a == 0 else 0)
        on_face = (level_id == lax.div(other, width * rows)) & on_x
        lines = jnp.concatenate(
            [jnp.where(on_face, theirs[a, m], 0.0) for m in range(MODES)], axis=0
        )
        high, low = halves(lines)
        lines = dot_nt(high, pick) + dot_nt(low, pick)
        for m in range(MODES):
            flux_x[a, m, 0:depth, :] = lines[m * depth : (m + 1) * depth]
            flux_x[a, m, HIGH + 1 :, :] = jnp.zeros((rows - 2, width), F32)
    flux_c[:, 4:, :] = jnp.zeros((2, rows - 4, width), F32)

    for copy in halo:
        copy.wait()

    columns = []
    for a in range(2):
        result = yh[a]
        for j, i in enumerate(Y_GROUP[a]):
            cx, _, cz = VELOCITY[i]
            if cx:
                own = (lane >= j * depth) & (lane < (j + 1) * depth)
                own = own & (sub == (0 if cx == 1 else rows - 1))
                result = jnp.where(own, yrh[a, SIGNS.index(cx)], result)
            if cz:
                place = j * depth if cz == 1 else (j + 1) * depth - 1
                result = jnp.where(lane == place, yzh[a, SIGNS.index(cz)], result)
        columns.append(result)
        column_out[a] = result
    for a in range(2):
        wrap = 0 if a == 0 else rows - 1
        for k, i in enumerate(X_GROUP[a]):
            cz = VELOCITY[i][2]
            first = (1 + cz) * rows + wrap
            pre[PLACE[i], pl.ds(first, depth, stride=rows), :] = xh[a, k]
            if cz:
                first = (1 if cz == 1 else depth) * rows + wrap
                pre[PLACE[i], first : first + 1, :] = xeh[a, SIGNS.index(cz)]
    for a in range(2):
        for j, i in enumerate(Y_GROUP[a]):
            if VELOCITY[i][0]:
                continue
            at_edge = lane == (0 if a == 0 else width - 1)
            for z in range(depth):
                tile_rows = pl.ds((z + 1) * rows, rows)
                place = j * depth + z
                column = jnp.broadcast_to(columns[a][:, place : place + 1], (rows, width))
                pre[PLACE[i], tile_rows] = jnp.where(at_edge, column, pre[PLACE[i], tile_rows])


    for copy in surfels[2:]:
        copy.wait()
    for a in range(2):
        for b in range(2):
            place = LOW if b == 0 else HIGH
            for m in range(MODES):
                flux_x[a, m, place : place + 1, :] = edges_in[a, b, m]
            for t in range(2):
                k = 2 * a + b
                flux_c[t, k : k + 1, :] = corners_in[a, b, t]

    total_out[...] = stage_sum(len(stages) - 1)


MOVED = X_GROUP[0] + X_GROUP[1]
FIXED_RUNS = ((0, 1), (3, 2), (5, 1), (6, 1), (15, 1), (16, 1), (17, 1), (18, 1))
MOVED_RUNS = ((1, 2), (7, 8))
N_CUTS = 4


def apply(pre, flux_m, flux_x, flux_y, flux_c, column, total, drive, out, force_out, amp_out, stage, force, amplitude, sem):
    depth, rows, width = flux_m.shape[1] - 2, flux_m.shape[2], flux_m.shape[3]
    copies = []

    def write(src, dst):
        copy = pltpu.make_async_copy(src, dst, sem.at[len(copies)])
        copy.start()
        copies.append(copy)

    for first, count in FIXED_RUNS:
        run = pl.ds(PLACE[first], count)
        write(pre.at[run, pl.ds(rows, depth * rows)], out.at[pl.ds(first, count)])

    lane = lax.broadcasted_iota(jnp.int32, (rows, width), 1)
    sub = lax.broadcasted_iota(jnp.int32, (rows, width), 0)
    load = total[:, :PANELS]
    force[...] = load
    write(force, force_out)
    amp = jnp.sum(drive[...] * load, axis=1, keepdims=True)
    diagonal = lax.broadcasted_iota(jnp.int32, (MODE_ROWS, MODES), 0) == lax.broadcasted_iota(
        jnp.int32, (MODE_ROWS, MODES), 1
    )
    amps = [jnp.broadcast_to(amp[m : m + 1], (rows, width)) for m in range(MODES)]
    groups = width // depth
    gains = []
    for t in range(2):
        gain = jnp.zeros((rows, width), F32)
        for m in range(t * groups, min(MODES, (t + 1) * groups)):
            gain = jnp.where(lane // depth == m - t * groups, amps[m], gain)
        gains.append(gain)

    def gather(first, second):
        tile = first * gains[0] + second * gains[1]
        step = depth
        while step < width:
            tile = tile + pltpu.roll(tile, step, 1)
            step *= 2
        return tile

    corner = gather(flux_c[0], flux_c[1])
    columns = {}
    for a, s in enumerate(SIGNS):
        face = gather(flux_y[a, 0], flux_y[a, 1])
        for b, t in enumerate(SIGNS):
            edge = corner[2 * a + b : 2 * a + b + 1]
            moved = pltpu.roll(face, t % rows, 0)
            moved = jnp.where(sub == (0 if t == 1 else rows - 1), edge, moved)
            i = VELOCITY.index((t, s, 0))
            columns[t, s] = column[a] + COEF[i] * moved

    def weigh(terms):
        return tree_sum([amps[m] * terms[m] for m in range(MODES)])

    lines = [
        [
            weigh([flux_x[a, m, r * rows : (r + 1) * rows, :] for m in range(MODES)])
            for r in range(3)
        ]
        for a in range(2)
    ]

    part = depth // N_CUTS
    for slot in range(depth + 2):
        flux = weigh([flux_m[m, slot] for m in range(MODES)])
        place = LOW if slot == 0 else HIGH if slot == depth + 1 else slot - 1
        for a, s in enumerate(SIGNS):
            line = lines[a][place // rows][place % rows : place % rows + 1]
            moved = pltpu.roll(flux, s % rows, 0)
            moved = jnp.where(sub == (0 if s == 1 else rows - 1), line, moved)
            for i in X_GROUP[a]:
                _, cy, cz = VELOCITY[i]
                z = slot - 1 + cz
                if not 0 <= z < depth:
                    continue
                value = pltpu.roll(moved, cy % width, 1) if cy else moved
                value = pre[PLACE[i], (z + 1) * rows : (z + 2) * rows, :] + COEF[i] * value
                if cy:
                    first = Y_GROUP[SIGNS.index(cy)].index(i) * depth + z
                    beside = columns[s, cy][:, first : first + 1]
                    beside = jnp.broadcast_to(beside, (rows, width))
                    value = jnp.where(lane == (0 if cy == 1 else width - 1), beside, value)
                stage[i, z * rows : (z + 1) * rows] = value
        if slot >= 2 and (slot - 1) % part == 0:
            cut = pl.ds((slot - 1 - part) * rows, part * rows)
            for first, count in MOVED_RUNS:
                run = pl.ds(first, count)
                write(stage.at[run, cut], out.at[run, cut])
    amplitude[...] = jnp.sum(jnp.where(diagonal, amp, 0.0), axis=0, keepdims=True)
    write(amplitude, amp_out)
    for copy in copies:
        copy.wait()


def per_device(sizes, pops, solid, cell, panel, area, shapes, panel_mode, compliance):
    depth, rows, width = pops.shape[1:]
    n_surf = cell.shape[-1]
    stages = stages_of(sizes)
    n_slots = max(len(stage_offsets(stage, sizes)) + 1 for stage in stages)
    vmem = pl.BlockSpec(memory_space=pltpu.VMEM)
    hbm = pl.BlockSpec(memory_space=pltpu.HBM)
    tile = (rows, width)
    dma = pltpu.SemaphoreType.DMA
    passed = pl.pallas_call(
        functools.partial(exchange, sizes),
        out_shape=(
            jax.ShapeDtypeStruct((19, (depth + 2) * rows, width), F32),
            jax.ShapeDtypeStruct((MODES, depth + 2) + tile, F32),
            jax.ShapeDtypeStruct((2, MODES, depth + rows, width), F32),
            jax.ShapeDtypeStruct((2, 2) + tile, F32),
            jax.ShapeDtypeStruct((2,) + tile, F32),
            jax.ShapeDtypeStruct((2,) + tile, F32),
            jax.ShapeDtypeStruct((1, width), F32),
            jax.ShapeDtypeStruct((MODE_ROWS, PANELS), F32),
        ),
        in_specs=[hbm] * 8,
        out_specs=(vmem,) * 8,
        scratch_shapes=[
            pltpu.VMEM(pops.shape, F32),
            pltpu.VMEM(solid.shape, jnp.int32),
            pltpu.VMEM((1, n_surf), jnp.int32),
            pltpu.VMEM((1, n_surf), jnp.int32),
            pltpu.VMEM((1, n_surf), F32),
            pltpu.VMEM((MODES, 1, n_surf), F32),
            pltpu.VMEM((1, PANELS), jnp.int32),
            pltpu.VMEM((1, MODES), F32),
            pltpu.VMEM((MODES + 1, 1, n_surf), F32),
            dma((7 + N_LOADS,)),
            pltpu.VMEM((19, depth * rows, width), F32),
            pltpu.VMEM((depth * rows, width), F32),
            pltpu.VMEM((2, 5, depth, width), F32),
            pltpu.VMEM((2, 5, depth, width), F32),
            pltpu.VMEM((2, 2, 1, width), F32),
            pltpu.VMEM((2, 2, 1, width), F32),
            pltpu.VMEM((2,) + tile, F32),
            pltpu.VMEM((2,) + tile, F32),
            pltpu.VMEM((2, 2, 1, width), F32),
            pltpu.VMEM((2, 2, 1, width), F32),
            pltpu.VMEM((2, 2) + tile, F32),
            pltpu.VMEM((2, MODES + 1, 1, n_surf), F32),
            pltpu.VMEM((2, 2, MODES, 1, width), F32),
            pltpu.VMEM((2, 2, MODES, 1, width), F32),
            pltpu.VMEM((2, 2) + tile, F32),
            pltpu.VMEM((2, 2, 2, 1, width), F32),
            pltpu.VMEM((2, 2, 2, 1, width), F32),
            dma((N_SURF,)),
            dma((N_SURF,)),
            pltpu.VMEM((len(stages), n_slots, 1, width), F32),
            dma((N_HALO,)),
            dma((N_HALO,)),
            dma((len(stages),)),
            dma((len(stages),)),
        ],
        compiler_params=pltpu.CompilerParams(
            collective_id=0, has_side_effects=True, vmem_limit_bytes=24 * 1024 * 1024
        ),
    )(
        *(
            pltpu.with_memory_space_constraint(x, pltpu.HBM)
            for x in (
                pops,
                solid,
                cell.reshape(1, n_surf),
                panel.reshape(1, n_surf),
                area.reshape(1, n_surf),
                shapes.reshape(MODES, 1, n_surf),
                panel_mode.reshape(1, PANELS),
                compliance.reshape(1, MODES),
            )
        )
    )
    read, force, amp = pl.pallas_call(
        apply,
        out_shape=(
            jax.ShapeDtypeStruct((19, depth * rows, width), F32),
            jax.ShapeDtypeStruct((1, PANELS), F32),
            jax.ShapeDtypeStruct((1, MODES), F32),
        ),
        in_specs=[vmem] * 8,
        out_specs=(hbm,) * 3,
        scratch_shapes=[
            pltpu.VMEM((19, depth * rows, width), F32),
            pltpu.VMEM((1, PANELS), F32),
            pltpu.VMEM((1, MODES), F32),
            dma((len(FIXED_RUNS) + len(MOVED_RUNS) * N_CUTS + 2,)),
        ],
        compiler_params=pltpu.CompilerParams(vmem_limit_bytes=8 * 1024 * 1024),
    )(*passed)
    return read.reshape(pops.shape), force.reshape(PANELS), amp.reshape(MODES)


def solution(mesh):
    placed = (
        P(None, "gz", "gx", "gy"),
        P("gz", "gx", "gy"),
        P("gz", "gx", "gy", None),
        P("gz", "gx", "gy", None),
        P("gz", "gx", "gy", None),
        P("gz", "gx", "gy", None, None),
        P(),
        P(),
    )
    return jax.shard_map(
        functools.partial(per_device, tuple(mesh.shape[a] for a in AXES)),
        mesh=mesh,
        in_specs=placed,
        out_specs=(P(None, "gz", "gx", "gy"), P(), P()),
        check_vma=False,
    )
```
